32 devices in a mesh: exp: 4 (over y, core), ctx: 8 (over z, x).
Axes of the slice: x: 2, y: 2, z: 4, core: 2. Of those that a mesh axis runs over, the one named last changes fastest.
Arguments:
- activations: bfloat16 [4, 1024, 768], P('exp', 'ctx'), may hold values from -6 to 6
- cotangent: bfloat16 [4, 1024, 768], P('exp', 'ctx'), may hold values from -6 to 6
- query_key_weight: bfloat16 [768, 1536], P(('exp', 'ctx')), may hold values from -0.109375 to 0.109375
- value_weight: bfloat16 [768, 768], P(('exp', 'ctx')), may hold values from -0.21875 to 0.21875
- output_weight: bfloat16 [768, 768], P(('exp', 'ctx')), may hold values from -0.875 to 0.875
- norm_first: bfloat16 [768], P(('exp', 'ctx')), may hold values from 0.5 to 1.5
- norm_second: bfloat16 [768], P(('exp', 'ctx')), may hold values from 0.5 to 1.5
- router_weight: bfloat16 [768, 4], P(('exp', 'ctx')), may hold values from -0.109375 to 0.109375
- bias_table: bfloat16 [32, 12], replicated, may hold values from -4 to 4
- w_in: bfloat16 [768, 4, 3072], P('ctx', 'exp'), may hold values from -0.21875 to 0.21875
- w_out: bfloat16 [3072, 4, 768], P('ctx', 'exp'), may hold values from -0.625 to 0.625
- routes: int32 [4, 1024], P('exp', 'ctx'), may hold values from 0 to 3, as said below
- slots: int32 [4, 1024], P('exp', 'ctx'), may hold values from 0 to 39, as said below
Outputs:
- layer_output: bfloat16 [4, 1024, 768], P('exp', 'ctx')
- grad_activations: bfloat16 [4, 1024, 768], P('exp', 'ctx')
- grad_qk: float32 [768, 1536], P(('exp', 'ctx'))
- grad_v: float32 [768, 768], P(('exp', 'ctx'))
- grad_o: float32 [768, 768], P(('exp', 'ctx'))
- grad_norm_first: float32 [768], P(('exp', 'ctx'))
- grad_norm_second: float32 [768], P(('exp', 'ctx'))
- grad_router: float32 [768, 4], P(('exp', 'ctx'))
- grad_table: float32 [32, 12], replicated
- grad_in: float32 [768, 4, 3072], P('ctx', 'exp')
- grad_out: float32 [3072, 4, 768], P('ctx', 'exp')
The draws below stay inside these ranges and needn't reach their ends.
Inputs may be any that keep to these rules, and one draw needn't show every extreme that they name: `routes`: within each aligned block of 128 tokens (the tokens of one device) no expert is named more than 40 times; in every block one expert is named exactly 40 times, the same expert for all 4 blocks at one position along the sequences. Tokens of one block that name the same expert have different slots.
All inputs are finite; a program needn't handle non-finite values.
Results may differ from the reference program's by a relative error of at most 0.024.
Values may be sent and summed in bfloat16 or wider, within the bound.
No kernel may reach another device: no remote copies, remote signals or barrier semaphores. Data moves between devices by JAX's collectives and lax.ppermute only.
A program may use at most 128 MiB of HBM per device.

```python
import jax
import jax.numpy as jnp
import numpy as np
from jax import lax

D = 768
H = 12
DH = 64
FF = 3072
NB = 32
TOK_DEV = 128
HD = 768
EXPERTS = 4
SEQS = 4
LENGTH = 1024
CAP = 40


def cell_table(key):
    blocks = SEQS * LENGTH // TOK_DEV
    positions = LENGTH // TOK_DEV
    cells = EXPERTS * CAP
    pick_key, block_key = jax.random.split(key)
    chosen = jax.random.randint(pick_key, (positions,), 0, EXPERTS)
    chosen_all = jnp.tile(chosen, SEQS)

    def one_block(block_seed, favoured):
        rank_key, shuffle_key = jax.random.split(block_seed)
        ranks = jax.random.permutation(rank_key, cells)
        cell_ids = jnp.arange(cells)
        scores = jnp.where(cell_ids // CAP == favoured, ranks, ranks + cells)
        ordering = jnp.argsort(scores)
        return jax.random.permutation(shuffle_key, ordering[:TOK_DEV])
    table = jax.vmap(one_block)(jax.random.split(block_key, blocks), chosen_all)
    return table.reshape(SEQS, LENGTH)


def draw_routes(key, part):
    table = cell_table(key)
    return (table // CAP).astype(jnp.int32)


def draw_slots(key, part):
    table = cell_table(key)
    return (table % CAP).astype(jnp.int32)


def steps_of(key, extent, cuts, low, high):
    def one(dim, blocks):
        draws = jax.random.uniform(jax.random.fold_in(jax.random.fold_in(key, 6), dim), (blocks,), jnp.float32, low / len(cuts), high / len(cuts))
        return jnp.repeat(jnp.exp(draws), extent[dim] // blocks).reshape((-1,) + (1,) * (len(extent) - dim - 1))

    level = one(*cuts[0])
    for cut in cuts[1:]:
        level = level * one(*cut)
    return level


def gaussian(rng, extent, deviation, bound, pieces=(), held_as=jnp.bfloat16):
    values = jax.random.normal(rng, extent, jnp.float32) * deviation
    if len(pieces) > 0:
        values = steps_of(rng, extent, pieces, -0.22, 0.18) * values
    return jnp.clip(values, min=-bound, max=bound).astype(held_as)


def setup_inputs(seed: int = 0) -> dict:
    arg_keys = jax.random.split(jax.random.key(seed), 14)
    return {
        "activations": gaussian(arg_keys[0], (SEQS, LENGTH, D), 1.0, 6.0, ((0, 4), (1, 8))),
        "cotangent": gaussian(arg_keys[1], (SEQS, LENGTH, D), 1.0, 6.0, ((0, 4), (1, 8))),
        "query_key_weight": gaussian(arg_keys[2], (D, 2 * HD), (4 * D) ** -0.5, 0.109375, ((0, 32),)),
        "value_weight": gaussian(arg_keys[3], (D, HD), D ** -0.5, 0.21875, ((0, 32),)),
        "output_weight": gaussian(arg_keys[4], (HD, D), (max(HD * 64 // LENGTH, 1)) ** -0.5, 0.875, ((0, 32),)),
        "norm_first": jnp.clip(1.0 + 0.1 * jax.random.normal(arg_keys[5], (D,), jnp.float32), 0.5, 1.5).astype(jnp.bfloat16),
        "norm_second": jnp.clip(1.0 + 0.1 * jax.random.normal(arg_keys[6], (D,), jnp.float32), 0.5, 1.5).astype(jnp.bfloat16),
        "router_weight": gaussian(arg_keys[7], (D, EXPERTS), (4 * D) ** -0.5, 0.109375, ((0, 32),)),
        "bias_table": gaussian(arg_keys[8], (NB, H), 1.0, 4.0),
        "w_in": gaussian(arg_keys[9], (D, EXPERTS, FF), D ** -0.5, 0.21875, ((0, 8), (1, 4))),
        "w_out": gaussian(arg_keys[10], (FF, EXPERTS, D), (FF // 36) ** -0.5, 0.625, ((0, 8), (1, 4))),
        "routes": draw_routes(jax.random.fold_in(arg_keys[13], 71), 0),
        "slots": draw_slots(jax.random.fold_in(arg_keys[13], 71), 0),
    }


EPS = 1e-06
TOP_PRECISION = lax.Precision.HIGHEST

@jax.custom_vjp
def reduced_copy(v):
    return lax.optimization_barrier(v.astype(jnp.bfloat16)).astype(jnp.float32)

@jax.custom_vjp
def reduced_backward(v):
    return v

def low_keep(v):
    return (reduced_copy(v), None)

def low_pass(kept, grad):
    return (grad,)

def back_keep(v):
    return (v, None)

def back_low(kept, grad):
    return (reduced_copy(grad),)
reduced_copy.defvjp(low_keep, low_pass)
reduced_backward.defvjp(back_keep, back_low)

def t5_buckets(length):
    relative = np.arange(-(length - 1), length)
    flipped = -relative
    result = np.where(flipped < 0, 16, 0)
    magnitude = np.abs(flipped)
    spread = 8 + (np.log(np.maximum(magnitude, 1) / 8.0) / np.log(16.0) * 8.0).astype(np.int64)
    spread = np.minimum(spread, 15)
    result = result + np.where(magnitude < 8, magnitude, spread)
    return jnp.asarray(result.astype(np.int32))

def rms_norm(hidden, gain):
    return hidden * lax.rsqrt(lax.optimization_barrier(jnp.mean(hidden * hidden, axis=-1, keepdims=True)) + EPS) * gain

def attend(queries, key_rows, value_rows, bias_table, bucket_table):
    block_rows = min(512, LENGTH)
    block_count = LENGTH // block_rows
    positions = jnp.arange(LENGTH, dtype=jnp.int32)

    def one_block(block_args):
        query_block, first_row = block_args
        query_pos = first_row + jnp.arange(block_rows, dtype=jnp.int32)
        offsets = positions[None, :] - query_pos[:, None] + (LENGTH - 1)
        bucket_ids = jnp.take(bucket_table, offsets)
        bias = jnp.transpose(jnp.take(bias_table, bucket_ids, axis=0), (2, 0, 1))
        scores = jnp.einsum('qhd,khd->hqk', query_block, key_rows, precision=TOP_PRECISION) + bias
        scores = reduced_backward(scores)
        chances = jax.nn.softmax(scores, axis=-1)
        return jnp.einsum('hqk,khd->qhd', reduced_copy(chances), value_rows, precision=TOP_PRECISION)
    blocks = queries.reshape(block_count, block_rows, H, DH)
    firsts = jnp.arange(block_count, dtype=jnp.int32) * block_rows
    attention_result = lax.map(jax.checkpoint(one_block), (blocks, firsts))
    return attention_result.reshape(LENGTH, H, DH)

def layer(activations, query_key_weight, value_weight, output_weight, norm_first, norm_second, router_weight, bias_table, w_in, w_out, routes, slots):
    bucket_table = t5_buckets(LENGTH)
    normalized_input = reduced_copy(rms_norm(activations, norm_first))
    output_projected = reduced_copy(reduced_backward(jnp.einsum('rnt,tc->rnc', normalized_input, query_key_weight, precision=TOP_PRECISION)))
    value_tensor = reduced_copy(reduced_backward(jnp.einsum('rnt,tc->rnc', normalized_input, value_weight, precision=TOP_PRECISION)))
    queries = output_projected[..., :HD].reshape(SEQS, LENGTH, H, DH)
    key_rows = output_projected[..., HD:].reshape(SEQS, LENGTH, H, DH)
    value_rows = value_tensor.reshape(SEQS, LENGTH, H, DH)
    attention_result = lax.map(lambda triple: attend(triple[0], triple[1], triple[2], bias_table, bucket_table), (queries, key_rows, value_rows))
    attention_result = reduced_copy(reduced_backward(attention_result.reshape(SEQS, LENGTH, HD)))
    hidden_middle = activations + reduced_backward(jnp.einsum('knb,bi->kni', attention_result, output_weight, precision=TOP_PRECISION))
    combined_output = reduced_copy(rms_norm(hidden_middle, norm_second))
    router_scores = reduced_backward(jnp.einsum('rnt,tc->rnc', combined_output, router_weight, precision=TOP_PRECISION))
    chances = jax.nn.softmax(router_scores, axis=-1)
    gate_value = jnp.take_along_axis(chances, routes[..., None], axis=-1)[..., 0]
    block_count = SEQS * LENGTH // TOK_DEV
    block_ids = jnp.broadcast_to(jnp.arange(block_count, dtype=jnp.int32)[:, None], (block_count, TOK_DEV))
    route_rows = routes.reshape(block_count, TOK_DEV)
    slot_rows = slots.reshape(block_count, TOK_DEV)
    buffer = jnp.zeros((block_count, EXPERTS, CAP, D), jnp.float32)
    buffer = buffer.at[block_ids, route_rows, slot_rows].set(combined_output.reshape(block_count, TOK_DEV, D))
    buffer = reduced_backward(buffer)
    preact = reduced_backward(jnp.einsum('becd,def->becf', buffer, w_in, precision=TOP_PRECISION))
    activated = reduced_copy(jax.nn.gelu(preact, approximate=False))
    produced = reduced_copy(reduced_backward(jnp.einsum('becf,fed->becd', activated, w_out, precision=TOP_PRECISION)))
    expert_rows = produced[block_ids, route_rows, slot_rows].reshape(SEQS, LENGTH, D)
    return hidden_middle + gate_value[..., None] * expert_rows

def reference(activations, cotangent, query_key_weight, value_weight, output_weight, norm_first, norm_second, router_weight, bias_table, w_in, w_out, routes, slots):
    floats = tuple((array.astype(jnp.float32) for array in (activations, query_key_weight, value_weight, output_weight, norm_first, norm_second, router_weight, bias_table, w_in, w_out)))

    def forward(*params):
        return layer(*params, routes, slots)
    result, pull = jax.vjp(forward, *floats)
    grads = pull(cotangent.astype(jnp.float32))
    return (result.astype(jnp.bfloat16), grads[0].astype(jnp.bfloat16), grads[1], grads[2], grads[3], grads[4], grads[5], grads[6], grads[7], grads[8], grads[9])
```

```python
import functools
import math

import jax
import jax.numpy as jnp
import numpy as np
from jax import lax
from jax.experimental import pallas as pl
from jax.experimental.pallas import tpu as pltpu
from jax.sharding import Mesh
from jax.sharding import PartitionSpec as P

EPS = 1e-06
F32 = jnp.float32
BF16 = jnp.bfloat16
EVERY = ("exp", "major", "minor")
VMEM_BYTES = 56 * 1024 * 1024


def bucket_edges(reach):
    magnitude = np.arange(reach)
    spread = 8 + (np.log(np.maximum(magnitude, 1) / 8.0) / np.log(16.0) * 8.0).astype(np.int64)
    bucket = np.where(magnitude < 8, magnitude, np.minimum(spread, 15))
    return [int(np.argmax(bucket >= number)) for number in range(16)]


def dot_t(left, right):
    return lax.dot_general(left, right, (((1,), (1,)), ((), ())), preferred_element_type=F32)


def dot_0(left, right):
    return lax.dot_general(left, right, (((0,), (0,)), ((), ())), preferred_element_type=F32)


def dot_n(left, right):
    return jnp.dot(left, right, preferred_element_type=F32)


def near_bias_kernel(edges, rows, table_ref, out_ref):
    shape = (3 * rows, rows)
    relative = (
        lax.broadcasted_iota(jnp.int32, shape, 0) - rows - lax.broadcasted_iota(jnp.int32, shape, 1)
    )
    magnitude = jnp.abs(relative)
    ahead = relative > 0
    for head in range(out_ref.shape[0]):
        value = jnp.where(ahead, table_ref[16, head], table_ref[0, head])
        for number in range(1, 16):
            value = jnp.where(
                magnitude >= edges[number],
                jnp.where(ahead, table_ref[16 + number, head], table_ref[number, head]),
                value,
            )
        out_ref[head] = value


def bucket_sum_kernel(edges, rows, near_ref, far_ref, out_ref):
    shape = (3 * rows, rows)
    relative = (
        lax.broadcasted_iota(jnp.int32, shape, 0) - rows - lax.broadcasted_iota(jnp.int32, shape, 1)
    )
    magnitude = jnp.abs(relative)
    lanes = lax.broadcasted_iota(jnp.int32, (1, 128), 1)
    for head in range(near_ref.shape[0]):
        grads = near_ref[head]
        behind = jnp.where(relative > 0, 0.0, grads)
        forward = jnp.where(relative > 0, grads, 0.0)
        total = jnp.zeros((1, 128), F32)
        for side, part in enumerate((behind, forward)):
            for number in range(16):
                inside = magnitude >= edges[number]
                if number < 15:
                    inside = inside & (magnitude < edges[number + 1])
                value = jnp.sum(jnp.sum(jnp.where(inside, part, 0.0), axis=0, keepdims=True))
                if number == 15:
                    value = value + jnp.sum(far_ref[head, side : side + 1, :])
                total = jnp.where(lanes == side * 16 + number, value, total)
        out_ref[head : head + 1, :] = total


def biased_scores(raw, far_ref, near_ref, scratch, head, block, rows):
    count = raw.shape[0]
    place = lax.broadcasted_iota(jnp.int32, raw.shape, 0)
    low, high = (block - 1) * rows, (block + 2) * rows
    far = jnp.where(
        place < low, far_ref[0, head], jnp.where(place >= high, far_ref[1, head], 0.0)
    )
    scratch[pl.ds(rows, count), :] = raw + far
    window = pl.ds(pl.multiple_of(block * rows, rows), 3 * rows)
    scratch[window, :] = scratch[window, :] + near_ref[head]
    return scratch[pl.ds(rows, count), :]


def attention_kernel(heads, rows, block_ref, far_ref, q_ref, kv_ref, near_ref, out_ref, lse_ref, scratch):
    block = block_ref[pl.program_id(0)]
    for head in range(heads):
        lanes = slice(head * 128, (head + 1) * 128)
        kv = kv_ref[:, lanes]
        scores = biased_scores(
            dot_t(kv, q_ref[:, lanes]), far_ref, near_ref, scratch.at[head % scratch.shape[0]], head, block, rows
        )
        top = jnp.max(scores, axis=0, keepdims=True)
        weights = jnp.exp(scores - top)
        total = jnp.sum(weights, axis=0, keepdims=True)
        low = (weights * (1.0 / total)).astype(BF16)
        out_ref[:, lanes] = dot_0(low, kv)
        lse_ref[0, head : head + 1, :] = top + jnp.log(total)


def attention_back_kernel(
    heads,
    rows,
    block_ref,
    far_ref,
    q_ref,
    g_ref,
    kv_ref,
    near_ref,
    lse_ref,
    delta_ref,
    dq_ref,
    dkv_ref,
    near_sum_ref,
    far_sum_ref,
    scratch,
    pad_scratch,
):
    step = pl.program_id(0)
    block = block_ref[step]
    count = kv_ref.shape[0]

    @pl.when(step == 0)
    def _():
        dkv_ref[...] = jnp.zeros_like(dkv_ref)
        near_sum_ref[...] = jnp.zeros_like(near_sum_ref)
        far_sum_ref[...] = jnp.zeros_like(far_sum_ref)
        for slot in range(pad_scratch.shape[0]):
            pad_scratch[slot, pl.ds(0, rows), :] = jnp.zeros((rows, rows), F32)
            pad_scratch[slot, pl.ds(rows + count, rows), :] = jnp.zeros((rows, rows), F32)

    place = lax.broadcasted_iota(jnp.int32, (count, rows), 0)
    low, high = (block - 1) * rows, (block + 2) * rows
    window = pl.ds(pl.multiple_of(block * rows, rows), 3 * rows)
    for head in range(heads):
        lanes = slice(head * 128, (head + 1) * 128)
        kv = kv_ref[:, lanes]
        both = jnp.concatenate([q_ref[:, lanes], g_ref[:, lanes]], axis=0)
        products = dot_t(kv, both)
        scores = biased_scores(
            products[:, :rows], far_ref, near_ref, scratch.at[head % scratch.shape[0]], head, block, rows
        )
        chances = jnp.exp(scores - lse_ref[0, head : head + 1, :])
        grads = chances * (products[:, rows:] - delta_ref[0, head : head + 1, :])
        grads_low = grads.astype(BF16)
        slot = head % pad_scratch.shape[0]
        pad_scratch[slot, pl.ds(rows, count), :] = grads
        near_sum_ref[head] += pad_scratch[slot, window, :]
        far_sum_ref[head, 0:1, :] += jnp.sum(jnp.where(place < low, grads, 0.0), axis=0, keepdims=True)
        far_sum_ref[head, 1:2, :] += jnp.sum(jnp.where(place >= high, grads, 0.0), axis=0, keepdims=True)
        pair = jnp.concatenate([grads_low, chances.astype(BF16)], axis=1)
        dkv_ref[:, lanes] += dot_n(pair, both)
        dq_ref[:, lanes] = dot_0(grads_low, kv).astype(BF16)


def whole_block(shape):
    zeros = (0,) * len(shape)
    return pl.BlockSpec(shape, lambda *_: zeros)


def scalars():
    return pl.BlockSpec(memory_space=pltpu.SMEM)


def slot_count(heads, count):
    return heads if count <= 2048 else 1


def forward_attention(queries, keys_values, near, far, blocks, heads, rows):
    count = keys_values.shape[0]
    steps = blocks.shape[0]
    width = heads * 128
    return pl.pallas_call(
        functools.partial(attention_kernel, heads, rows),
        grid=(steps,),
        in_specs=[
            scalars(),
            scalars(),
            pl.BlockSpec((rows, width), lambda i: (i, 0)),
            whole_block((count, width)),
            whole_block(near.shape),
        ],
        out_specs=[
            pl.BlockSpec((rows, width), lambda i: (i, 0)),
            pl.BlockSpec((1, heads, rows), lambda i: (i, 0, 0)),
        ],
        out_shape=[
            jax.ShapeDtypeStruct((steps * rows, width), F32),
            jax.ShapeDtypeStruct((steps, heads, rows), F32),
        ],
        scratch_shapes=[pltpu.VMEM((slot_count(heads, count), count + 2 * rows, rows), F32)],
        compiler_params=pltpu.CompilerParams(vmem_limit_bytes=VMEM_BYTES),
        cost_estimate=pl.CostEstimate(
            flops=4 * steps * rows * count * width, bytes_accessed=8 * count * width, transcendentals=steps * rows * count * heads
        ),
    )(blocks, far, queries, keys_values, near)


def backward_attention(queries, grads, keys_values, near, far, blocks, lse, delta, heads, rows):
    count = keys_values.shape[0]
    steps = blocks.shape[0]
    width = heads * 128
    row_spec = pl.BlockSpec((1, heads, rows), lambda i: (i, 0, 0))
    return pl.pallas_call(
        functools.partial(attention_back_kernel, heads, rows),
        grid=(steps,),
        in_specs=[
            scalars(),
            scalars(),
            pl.BlockSpec((rows, width), lambda i: (i, 0)),
            pl.BlockSpec((rows, width), lambda i: (i, 0)),
            whole_block((count, width)),
            whole_block(near.shape),
            row_spec,
            row_spec,
        ],
        out_specs=[
            pl.BlockSpec((rows, width), lambda i: (i, 0)),
            whole_block((count, width)),
            whole_block(near.shape),
            whole_block((heads, 2, rows)),
        ],
        out_shape=[
            jax.ShapeDtypeStruct((steps * rows, width), BF16),
            jax.ShapeDtypeStruct((count, width), F32),
            jax.ShapeDtypeStruct(near.shape, F32),
            jax.ShapeDtypeStruct((heads, 2, rows), F32),
        ],
        scratch_shapes=[
            pltpu.VMEM((slot_count(heads, count), count + 2 * rows, rows), F32),
            pltpu.VMEM((slot_count(heads, count), count + 2 * rows, rows), F32),
        ],
        compiler_params=pltpu.CompilerParams(vmem_limit_bytes=VMEM_BYTES),
        cost_estimate=pl.CostEstimate(
            flops=10 * steps * rows * count * width, bytes_accessed=8 * count * width, transcendentals=steps * rows * count * heads
        ),
    )(blocks, far, queries, grads, keys_values, near, lse, delta)


def swap_pairs():
    return [(0, 1), (1, 0)]


def gather_minor(value):
    count = lax.axis_size("minor")
    if count != 2:
        return lax.all_gather(value, "minor")
    other = lax.ppermute(value, "minor", swap_pairs())
    first = lax.axis_index("minor") == 0
    return jnp.stack([jnp.where(first, value, other), jnp.where(first, other, value)])


def sum_minor(parts):
    count = lax.axis_size("minor")
    if count != 2:
        arrived = lax.all_to_all(parts.astype(BF16), "minor", 0, 0, tiled=True)
        return jnp.sum(arrived.astype(F32), axis=0)
    first = lax.axis_index("minor") == 0
    sent = jnp.where(first, parts[1], parts[0]).astype(BF16)
    return jnp.where(first, parts[0], parts[1]) + lax.ppermute(sent, "minor", swap_pairs()).astype(F32)


def swap_major(value):
    return lax.all_to_all(value, "major", 0, 0, tiled=True)


def unit(hidden):
    return lax.rsqrt(jnp.mean(hidden * hidden, axis=-1, keepdims=True) + EPS)


def per_device(
    activations,
    cotangent,
    query_key_weight,
    value_weight,
    output_weight,
    norm_first,
    norm_second,
    router_weight,
    bias_table,
    w_in,
    w_out,
    routes,
    slots,
):
    rows, width = activations.shape[1:]
    major = lax.axis_size("major")
    minor = lax.axis_size("minor")
    groups = lax.axis_size("exp")
    devices = groups * major * minor
    experts = router_weight.shape[1]
    capacity = rows * 5 // (4 * experts)
    head_count = bias_table.shape[1]
    heads = head_count // major
    features = value_weight.shape[1]
    head_dim = features // head_count
    shard = query_key_weight.shape[0]
    my_major = lax.axis_index("major")
    my_minor = lax.axis_index("minor")
    my_exp = lax.axis_index("exp")
    edges = bucket_edges(4 * rows)
    kv_width = heads * 2 * head_dim
    q_width = heads * head_dim
    extra_width = 128 - (kv_width + q_width) % 128
    packed_width = kv_width + q_width + extra_width

    column = swap_major(jnp.broadcast_to(activations, (major, rows, width)))

    def by_head(value):
        return value.reshape(shard, major, heads, 1, head_dim)

    key_value = jnp.concatenate(
        [by_head(query_key_weight[:, features:]), by_head(value_weight)], axis=3
    ).reshape(shard, major, kv_width)
    extras = jnp.concatenate([router_weight, norm_first[:, None], norm_second[:, None]], axis=1)
    extras = jnp.pad(extras, ((0, 0), (0, extra_width - experts - 2)))
    packed = jnp.concatenate(
        [
            key_value,
            query_key_weight[:, :features].reshape(shard, major, q_width),
            jnp.broadcast_to(extras[:, None, :], (shard, major, extra_width)),
        ],
        axis=2,
    )
    packed = swap_major(jnp.transpose(packed, (1, 0, 2)))
    packed = gather_minor(packed)
    packed = lax.all_gather(packed, "exp")
    packed = jnp.transpose(packed, (0, 2, 1, 3, 4)).reshape(width, packed_width)
    extras = packed[:, kv_width + q_width :]
    full_router = extras[:, :experts]
    gain_first = extras[:, experts].astype(F32)
    gain_second = extras[:, experts + 1].astype(F32)
    head_weight = packed[:, : kv_width + q_width]

    full_o = lax.all_gather(output_weight, EVERY, axis=0, tiled=True)

    table = lax.dynamic_slice_in_dim(bias_table, my_major * heads, heads, axis=1).astype(F32)
    near = pl.pallas_call(
        functools.partial(near_bias_kernel, edges, rows),
        in_specs=[scalars()],
        out_shape=jax.ShapeDtypeStruct((heads, 3 * rows, rows), F32),
    )(table)
    far = jnp.stack([table[15], table[31]])
    blocks = jnp.arange(major, dtype=jnp.int32) * minor + my_minor

    quarter = w_in.shape[2] // major
    inner = swap_major(jnp.transpose(w_in.reshape(w_in.shape[0], major, quarter), (1, 0, 2)))
    outer = w_out[:, 0, :]
    both = gather_minor(jnp.concatenate([inner.reshape(-1, width), outer], axis=0))
    inner = both[:, : width // minor].reshape(minor, major, width // devices * groups, quarter)
    inner = jnp.transpose(inner, (1, 0, 2, 3)).reshape(width, quarter)
    outer = both[:, width // minor :].reshape(quarter, width)

    expert_ids = jnp.arange(experts, dtype=jnp.int32)
    slot_ids = jnp.arange(capacity, dtype=jnp.int32)
    select = (
        (routes[0][None, None, :] == expert_ids[:, None, None])
        & (slots[0][None, None, :] == slot_ids[None, :, None])
    ).astype(BF16)
    select = select.reshape(experts * capacity, rows)

    def dispatch(value):
        sent = dot_n(select, value).astype(BF16).reshape(groups, 1, capacity, width)
        sent = jnp.broadcast_to(sent, (groups, major, capacity, width))
        sent = sent.reshape(groups * major, capacity, width)
        arrived = lax.all_to_all(sent, ("exp", "major"), 0, 0, tiled=True)
        return arrived.reshape(groups * major * capacity, width)

    def give_back(value):
        arrived = lax.all_to_all(
            value.astype(BF16).reshape(groups * major, capacity, width), ("exp", "major"), 0, 0, tiled=True
        )
        arrived = jnp.sum(arrived.reshape(groups, major, capacity, width).astype(F32), axis=1)
        return dot_0(select, arrived.astype(BF16).reshape(experts * capacity, width))

    sent = dot_n(select, cotangent[0]).astype(BF16).reshape(groups, capacity, width)
    sent = lax.all_to_all(sent, "exp", 0, 0, tiled=True)
    cot_rows = lax.all_gather(sent, "major", axis=1).reshape(groups * major * capacity, width)

    column_hidden = column.reshape(major * rows, width).astype(F32)
    column_unit = unit(column_hidden)
    normed = (column_hidden * column_unit * gain_first).astype(BF16)
    projected = dot_n(normed, head_weight).astype(BF16)
    kv_own = projected[:, :kv_width].reshape(major, rows, kv_width)
    keys_values = jnp.transpose(gather_minor(kv_own), (1, 0, 2, 3)).reshape(-1, kv_width)
    queries = projected[:, kv_width:].reshape(major * rows, heads, head_dim)
    queries = jnp.pad(queries, ((0, 0), (0, 0), (0, head_dim))).reshape(major * rows, kv_width)
    attended_wide, lse = forward_attention(queries, keys_values, near, far, blocks, heads, rows)
    attended_heads = attended_wide.reshape(major * rows, heads, 2, head_dim)[:, :, 1, :]
    attended = swap_major(attended_heads.astype(BF16).reshape(major, rows, q_width))
    attended = jnp.transpose(attended, (1, 0, 2)).reshape(rows, features)

    hidden = activations[0].astype(F32)
    middle = hidden + dot_n(attended, full_o)
    middle_unit = unit(middle)
    mixed = (middle * middle_unit * gain_second).astype(BF16)
    chances = jax.nn.softmax(dot_n(mixed, full_router), axis=-1)
    route_mask = (routes[0][:, None] == expert_ids[None, :]).astype(F32)
    gate = jnp.sum(chances * route_mask, axis=-1, keepdims=True)

    buffer = dispatch(mixed)
    row_chances = jax.nn.softmax(dot_n(buffer, full_router), axis=-1)
    row_mask = (expert_ids == my_exp).astype(F32)[None, :]
    row_gate = jnp.sum(row_chances * row_mask, axis=-1, keepdims=True)
    preact = dot_n(buffer, inner)
    cumulative = 0.5 * (1.0 + lax.erf(preact * math.sqrt(0.5)))
    density = jnp.exp(-0.5 * preact * preact) * (1.0 / math.sqrt(2.0 * math.pi))
    activated_wide = preact * cumulative
    grad_activated = dot_t(cot_rows, outer)
    grad_preact = (row_gate * grad_activated * (cumulative + preact * density)).astype(BF16)
    row_grad_gate = jnp.sum(activated_wide * grad_activated, axis=-1, keepdims=True)
    grad_logits = (row_gate * row_grad_gate * (row_mask - row_chances)).astype(BF16)
    grad_mixed = give_back(dot_t(grad_preact, inner) + dot_t(grad_logits, full_router))

    activated = activated_wide.astype(BF16)
    produced = give_back(dot_n(activated, outer))
    layer_output = (middle + gate * produced).astype(BF16)[None]
    grad_router = dot_0(buffer, grad_logits)
    gated_rows = (row_gate * cot_rows.astype(F32)).astype(BF16)
    grad_outer = dot_0(activated, gated_rows).reshape(minor, -1, width)
    grad_inner = dot_0(buffer, grad_preact).reshape(major, minor, -1, quarter)
    grad_inner = jnp.transpose(grad_inner, (1, 0, 2, 3)).reshape(minor, -1, quarter)
    grad_both = sum_minor(jnp.concatenate([grad_inner, grad_outer], axis=1))
    grad_outer = grad_both[width // minor :][:, None, :]
    grad_inner = swap_major(grad_both[: width // minor].astype(BF16).reshape(major, -1, quarter))
    grad_inner = jnp.transpose(grad_inner, (1, 0, 2)).reshape(-1, 1, major * quarter).astype(F32)

    grad_z = cotangent[0].astype(F32)
    grad_gain_second = jnp.sum(grad_mixed * middle * middle_unit, axis=0)
    scaled = grad_mixed * gain_second
    grad_middle = (
        grad_z
        + middle_unit * scaled
        - middle * middle_unit**3 * jnp.mean(scaled * middle, axis=-1, keepdims=True)
    )
    grad_branch = grad_middle.astype(BF16)
    grad_attended = dot_t(grad_branch, full_o).astype(BF16)
    grad_attended = swap_major(
        jnp.transpose(grad_attended.reshape(rows, major, q_width), (1, 0, 2))
    ).reshape(major * rows, heads, head_dim)
    grad_o = dot_0(attended, grad_branch).astype(BF16).reshape(devices, shard, width)
    grad_o = jnp.sum(lax.all_to_all(grad_o, EVERY, 0, 0, tiled=True).astype(F32), axis=0)

    delta = jnp.sum(grad_attended.astype(F32) * attended_heads, axis=-1)
    delta = jnp.transpose(delta.reshape(major, rows, heads), (0, 2, 1))
    grad_wide = jnp.pad(grad_attended, ((0, 0), (0, 0), (head_dim, 0))).reshape(-1, kv_width)
    dq_wide, dkv, near_sum, far_sum = backward_attention(
        queries, grad_wide, keys_values, near, far, blocks, lse, delta, heads, rows
    )
    sums = pl.pallas_call(
        functools.partial(bucket_sum_kernel, edges, rows),
        out_shape=jax.ShapeDtypeStruct((heads, 128), F32),
    )(near_sum, far_sum)
    grad_table = sums[:, :32].T
    dkv = jnp.transpose(dkv.reshape(major, minor, rows, kv_width), (1, 0, 2, 3))
    dkv = sum_minor(dkv).reshape(major * rows, kv_width).astype(BF16)
    dq = dq_wide.reshape(major * rows, heads, 2, head_dim)[:, :, 0, :].reshape(-1, q_width)
    grad_projected = jnp.concatenate([dkv, dq], axis=1)

    grad_normed = dot_t(grad_projected, head_weight)
    grad_gain_first = jnp.sum(grad_normed * column_hidden * column_unit, axis=0)
    grad_normed = swap_major(grad_normed.astype(BF16).reshape(major, rows, width))
    grad_normed = jnp.sum(grad_normed.astype(F32), axis=0)
    hidden_unit = unit(hidden)
    scaled = grad_normed * gain_first
    grad_activations = (
        grad_middle
        + hidden_unit * scaled
        - hidden * hidden_unit**3 * jnp.mean(scaled * hidden, axis=-1, keepdims=True)
    ).astype(BF16)[None]

    grad_weight = dot_0(normed, grad_projected).astype(BF16).reshape(devices, shard, -1)
    small = jnp.concatenate(
        [grad_router, grad_gain_first[:, None], grad_gain_second[:, None]], axis=1
    ).reshape(devices, shard, experts + 2)
    buckets = bias_table.shape[0]
    table_columns = buckets * heads // shard
    flat_table = jnp.broadcast_to(
        grad_table.reshape(1, shard, table_columns), (devices, shard, table_columns)
    )
    spare = extra_width - experts - 2 - table_columns
    sent = jnp.concatenate(
        [
            grad_weight,
            small.astype(BF16),
            flat_table.astype(BF16),
            jnp.zeros((devices, shard, spare), BF16),
        ],
        axis=2,
    )
    arrived = lax.all_to_all(sent, EVERY, 0, 0, tiled=True).astype(F32)
    arrived = jnp.sum(arrived.reshape(groups, major, minor, shard, packed_width), axis=(0, 2))
    key_value = arrived[:, :, :kv_width].reshape(major, shard, heads, 2, head_dim)

    def side_by_side(value):
        return jnp.transpose(value.reshape(major, shard, q_width), (1, 0, 2)).reshape(shard, features)

    grad_query = side_by_side(arrived[:, :, kv_width : kv_width + q_width])
    grad_key = side_by_side(key_value[:, :, :, 0, :])
    grad_v = side_by_side(key_value[:, :, :, 1, :])
    small = arrived[:, :, kv_width + q_width :]
    summed = jnp.sum(small[:, :, : experts + 2], axis=0)
    grad_table = small[:, :, experts + 2 : experts + 2 + table_columns]
    grad_table = jnp.transpose(grad_table.reshape(major, buckets, heads), (1, 0, 2))
    return (
        layer_output,
        grad_activations,
        jnp.concatenate([grad_query, grad_key], axis=1),
        grad_v,
        grad_o,
        summed[:, experts],
        summed[:, experts + 1],
        summed[:, :experts],
        grad_table.reshape(buckets, head_count),
        grad_inner,
        grad_outer,
    )


def solution(mesh):
    groups, ring = mesh.shape["exp"], mesh.shape["ctx"]
    major = math.gcd(ring, 4)
    split = Mesh(mesh.devices.reshape(groups, major, ring // major), EVERY)
    ctx = ("major", "minor")
    tokens, rows, experts = P("exp", ctx, None), P(EVERY, None), P(ctx, "exp", None)
    return jax.shard_map(
        per_device,
        mesh=split,
        in_specs=(
            tokens,
            tokens,
            rows,
            rows,
            rows,
            P(EVERY),
            P(EVERY),
            rows,
            P(),
            experts,
            experts,
            P("exp", ctx),
            P("exp", ctx),
        ),
        out_specs=(
            tokens,
            tokens,
            rows,
            rows,
            rows,
            P(EVERY),
            P(EVERY),
            rows,
            P(),
            experts,
            experts,
        ),
        check_vma=False,
    )
```

```python
import functools
import math

import jax
import jax.numpy as jnp
import numpy as np
from jax import lax
from jax.experimental import pallas as pl
from jax.experimental.pallas import tpu as pltpu
from jax.sharding import Mesh
from jax.sharding import PartitionSpec as P

EPS = 1e-06
F32 = jnp.float32
BF16 = jnp.bfloat16
EVERY = ("ey", "ec", "gh", "mj", "rs")
MINOR = ("ec", "rs")
REST = ("ey", "gh", "mj", "rs")
VMEM_BYTES = 56 * 1024 * 1024


def bucket_edges(reach):
    magnitude = np.arange(reach)
    spread = 8 + (np.log(np.maximum(magnitude, 1) / 8.0) / np.log(16.0) * 8.0).astype(np.int64)
    bucket = np.where(magnitude < 8, magnitude, np.minimum(spread, 15))
    return [int(np.argmax(bucket >= number)) for number in range(16)]


def dot_t(left, right):
    return lax.dot_general(left, right, (((1,), (1,)), ((), ())), preferred_element_type=F32)


def dot_0(left, right):
    return lax.dot_general(left, right, (((0,), (0,)), ((), ())), preferred_element_type=F32)


def dot_n(left, right):
    return jnp.dot(left, right, preferred_element_type=F32)


def near_bias_kernel(edges, rows, table_ref, out_ref):
    shape = (3 * rows, rows)
    relative = (
        lax.broadcasted_iota(jnp.int32, shape, 0) - rows - lax.broadcasted_iota(jnp.int32, shape, 1)
    )
    magnitude = jnp.abs(relative)
    ahead = relative > 0
    for head in range(out_ref.shape[0]):
        value = jnp.where(ahead, table_ref[16, head], table_ref[0, head])
        for number in range(1, 16):
            value = jnp.where(
                magnitude >= edges[number],
                jnp.where(ahead, table_ref[16 + number, head], table_ref[number, head]),
                value,
            )
        out_ref[head] = value


def bucket_sum_kernel(edges, rows, near_ref, far_ref, out_ref):
    shape = (3 * rows, rows)
    relative = (
        lax.broadcasted_iota(jnp.int32, shape, 0) - rows - lax.broadcasted_iota(jnp.int32, shape, 1)
    )
    magnitude = jnp.abs(relative)
    lanes = lax.broadcasted_iota(jnp.int32, (1, 128), 1)
    for head in range(near_ref.shape[0]):
        grads = near_ref[head]
        behind = jnp.where(relative > 0, 0.0, grads)
        forward = jnp.where(relative > 0, grads, 0.0)
        total = jnp.zeros((1, 128), F32)
        for side, part in enumerate((behind, forward)):
            for number in range(16):
                inside = magnitude >= edges[number]
                if number < 15:
                    inside = inside & (magnitude < edges[number + 1])
                value = jnp.sum(jnp.sum(jnp.where(inside, part, 0.0), axis=0, keepdims=True))
                if number == 15:
                    value = value + jnp.sum(far_ref[head, side : side + 1, :])
                total = jnp.where(lanes == side * 16 + number, value, total)
        out_ref[head : head + 1, :] = total


def biased_scores(parts, key_ref, place_ref, far_ref, near_ref, scratch, head, block, rows):
    pieces = [
        part[first : first + rows, :] for part in parts for first in range(0, part.shape[0], rows)
    ]
    slots = len(pieces)
    for slot in range(slots):
        far = jnp.where(
            key_ref[slot] < block - 1,
            far_ref[0, head],
            jnp.where(key_ref[slot] > block + 1, far_ref[1, head], 0.0),
        )
        scratch[slot * rows : (slot + 1) * rows, :] = pieces[slot] + far
    for step in range(3):
        window = pl.ds(pl.multiple_of(place_ref[block + step] * rows, rows), rows)
        scratch[window, :] = scratch[window, :] + near_ref[head, step * rows : (step + 1) * rows, :]
    return scratch[0 : slots * rows, :]


def head_queries(q_ref, heads, head):
    first = heads * 128 + head * 64
    query = q_ref[:, first : first + 64]
    return jnp.concatenate([query, jnp.zeros_like(query)], axis=1)


def attention_kernel(
    heads,
    rows,
    block_ref,
    key_ref,
    place_ref,
    far_ref,
    q_ref,
    own_ref,
    other_ref,
    near_ref,
    low_ref,
    wide_ref,
    lse_ref,
    scratch,
):
    block = block_ref[pl.program_id(0)]
    own_rows = own_ref.shape[0]
    for head in range(heads):
        lanes = slice(head * 128, (head + 1) * 128)
        own, other = own_ref[:, lanes], other_ref[:, lanes]
        query = head_queries(q_ref, heads, head)
        scores = biased_scores(
            (dot_t(own, query), dot_t(other, query)),
            key_ref,
            place_ref,
            far_ref,
            near_ref,
            scratch.at[head % scratch.shape[0]],
            head,
            block,
            rows,
        )
        top = jnp.max(scores, axis=0, keepdims=True)
        weights = jnp.exp(scores - top)
        total = jnp.sum(weights, axis=0, keepdims=True)
        low = (weights * (1.0 / total)).astype(BF16)
        result = dot_0(low[:own_rows], own) + dot_0(low[own_rows:], other)
        wide_ref[:, lanes] = result
        low_ref[:, head * 64 : (head + 1) * 64] = result[:, 64:].astype(BF16)
        lse_ref[0, head : head + 1, :] = top + jnp.log(total)


def attention_back_kernel(
    heads,
    rows,
    block_ref,
    key_ref,
    place_ref,
    far_ref,
    q_ref,
    g_ref,
    wide_ref,
    own_ref,
    other_ref,
    near_ref,
    lse_ref,
    dq_ref,
    sum_ref,
    low_ref,
    near_sum_ref,
    far_sum_ref,
    scratch,
    grad_scratch,
    total_scratch,
):
    step = pl.program_id(0)
    block = block_ref[step]
    own_rows = own_ref.shape[0]
    count = own_rows + other_ref.shape[0]
    slots = count // rows

    @pl.when(step == 0)
    def _():
        total_scratch[...] = jnp.zeros_like(total_scratch)
        near_sum_ref[...] = jnp.zeros_like(near_sum_ref)
        far_sum_ref[...] = jnp.zeros_like(far_sum_ref)
        for copy in range(grad_scratch.shape[0]):
            grad_scratch[copy, count : count + rows, :] = jnp.zeros((rows, rows), F32)

    for head in range(heads):
        copy = head % scratch.shape[0]
        lanes = slice(head * 128, (head + 1) * 128)
        own, other = own_ref[:, lanes], other_ref[:, lanes]
        grad = g_ref[:, head * 64 : (head + 1) * 64]
        grad = jnp.concatenate([jnp.zeros_like(grad), grad], axis=1)
        delta = jnp.sum(jnp.transpose(grad.astype(F32) * wide_ref[:, lanes]), axis=0, keepdims=True)
        both = jnp.concatenate([head_queries(q_ref, heads, head), grad], axis=0)
        first, second = dot_t(own, both), dot_t(other, both)
        scores = biased_scores(
            (first[:, :rows], second[:, :rows]),
            key_ref,
            place_ref,
            far_ref,
            near_ref,
            scratch.at[copy],
            head,
            block,
            rows,
        )
        chances = jnp.exp(scores - lse_ref[0, head : head + 1, :])
        products = jnp.concatenate([first[:, rows:], second[:, rows:]], axis=0)
        grads = chances * (products - delta)
        grads_low = grads.astype(BF16)
        grad_scratch[copy, 0:count, :] = grads
        for part in range(3):
            window = pl.ds(pl.multiple_of(place_ref[block + part] * rows, rows), rows)
            near_sum_ref[head, part * rows : (part + 1) * rows, :] += grad_scratch[copy, window, :]
        low_far = jnp.zeros((1, rows), F32)
        high_far = jnp.zeros((1, rows), F32)
        for slot in range(slots):
            line = jnp.sum(grads[slot * rows : (slot + 1) * rows, :], axis=0, keepdims=True)
            low_far = low_far + line * jnp.where(key_ref[slot] < block - 1, 1.0, 0.0)
            high_far = high_far + line * jnp.where(key_ref[slot] > block + 1, 1.0, 0.0)
        far_sum_ref[head, 0:1, :] += low_far
        far_sum_ref[head, 1:2, :] += high_far
        pair = jnp.concatenate([grads_low, chances.astype(BF16)], axis=1)
        total_scratch[:, lanes] += dot_n(pair, both)
        dq = dot_0(grads_low[:own_rows], own) + dot_0(grads_low[own_rows:], other)
        dq_ref[:, head * 64 : (head + 1) * 64] = dq[:, :64].astype(BF16)

    dq_ref[:, heads * 64 :] = jnp.zeros_like(dq_ref[:, heads * 64 :])

    @pl.when(step == pl.num_programs(0) - 1)
    def _():
        sum_ref[...] = total_scratch[0:own_rows, :]
        low_ref[...] = total_scratch[own_rows:count, :].astype(BF16)


def unpack_kernel(cuts, in_ref, out_ref):
    count = in_ref.shape[0]
    step = in_ref.shape[2] // cuts
    for cut in range(cuts):
        for index in range(count):
            first = (cut * count + index) * step
            value = in_ref[index, :, cut * step : (cut + 1) * step].astype(F32)
            out_ref[:, 0, first : first + step] = value


def unpack(value, cuts):
    count, rows, columns = value.shape
    return pl.pallas_call(
        functools.partial(unpack_kernel, cuts),
        out_shape=jax.ShapeDtypeStruct((rows, 1, count * columns), F32),
    )(value)


def whole_block(shape):
    zeros = (0,) * len(shape)
    return pl.BlockSpec(shape, lambda *_: zeros)


def scalars():
    return pl.BlockSpec(memory_space=pltpu.SMEM)


def slot_count(heads, count):
    return heads if count <= 2048 else 1


def estimate(products, steps, rows, count, heads):
    return pl.CostEstimate(
        flops=2 * products * steps * rows * count * heads * 128,
        bytes_accessed=1024 * count * heads,
        transcendentals=steps * rows * count * heads,
    )


def forward_attention(projected, other, near, far, places, heads, rows):
    steps = places[0].shape[0]
    own = steps * rows
    count = own + other.shape[0]
    width = heads * 128
    return pl.pallas_call(
        functools.partial(attention_kernel, heads, rows),
        grid=(steps,),
        in_specs=[scalars()] * 4
        + [
            pl.BlockSpec((rows, projected.shape[1]), lambda i: (i, 0)),
            whole_block((own, width)),
            whole_block((count - own, width)),
            whole_block(near.shape),
        ],
        out_specs=[
            pl.BlockSpec((rows, width // 2), lambda i: (i, 0)),
            pl.BlockSpec((rows, width), lambda i: (i, 0)),
            pl.BlockSpec((1, heads, rows), lambda i: (i, 0, 0)),
        ],
        out_shape=[
            jax.ShapeDtypeStruct((own, width // 2), BF16),
            jax.ShapeDtypeStruct((own, width), F32),
            jax.ShapeDtypeStruct((steps, heads, rows), F32),
        ],
        scratch_shapes=[pltpu.VMEM((slot_count(heads, count), count + rows, rows), F32)],
        compiler_params=pltpu.CompilerParams(vmem_limit_bytes=VMEM_BYTES),
        cost_estimate=estimate(2, steps, rows, count, heads),
    )(*places, far, projected, projected, other, near)


def backward_attention(projected, grads, wide, other, near, far, places, lse, heads, rows):
    steps = places[0].shape[0]
    own = steps * rows
    count = own + other.shape[0]
    width = heads * 128
    dq_width = -(-width // 256) * 128
    slots = slot_count(heads, count)
    return pl.pallas_call(
        functools.partial(attention_back_kernel, heads, rows),
        grid=(steps,),
        in_specs=[scalars()] * 4
        + [
            pl.BlockSpec((rows, projected.shape[1]), lambda i: (i, 0)),
            pl.BlockSpec((rows, width // 2), lambda i: (i, 0)),
            pl.BlockSpec((rows, width), lambda i: (i, 0)),
            whole_block((own, width)),
            whole_block((count - own, width)),
            whole_block(near.shape),
            pl.BlockSpec((1, heads, rows), lambda i: (i, 0, 0)),
        ],
        out_specs=[
            pl.BlockSpec((rows, dq_width), lambda i: (i, 0)),
            whole_block((own, width)),
            whole_block((count - own, width)),
            whole_block(near.shape),
            whole_block((heads, 2, rows)),
        ],
        out_shape=[
            jax.ShapeDtypeStruct((own, dq_width), BF16),
            jax.ShapeDtypeStruct((own, width), F32),
            jax.ShapeDtypeStruct((count - own, width), BF16),
            jax.ShapeDtypeStruct(near.shape, F32),
            jax.ShapeDtypeStruct((heads, 2, rows), F32),
        ],
        scratch_shapes=[
            pltpu.VMEM((slots, count + rows, rows), F32),
            pltpu.VMEM((slots, count + rows, rows), F32),
            pltpu.VMEM((count, width), F32),
        ],
        compiler_params=pltpu.CompilerParams(vmem_limit_bytes=VMEM_BYTES),
        cost_estimate=estimate(5, steps, rows, count, heads),
    )(*places, far, projected, grads, wide, projected, other, near, lse)


def swap(value, axis):
    return lax.ppermute(value, axis, [(0, 1), (1, 0)])


def turn(value):
    return lax.ppermute(value, ("ec", "gh"), [(0, 0), (1, 2), (2, 1), (3, 3)])


def exchange(parts, axis):
    count = len(parts)
    return [parts[0]] + [
        lax.ppermute(parts[step], axis, [(source, source ^ step) for source in range(count)])
        for step in range(1, count)
    ]


def ordered(value, place):
    count = value.shape[0]
    return jnp.take(value, jnp.arange(count) ^ place, axis=0, mode="clip")


def exchange_ordered(value, axis):
    place = lax.axis_index(axis)
    count = value.shape[0]
    parts = exchange(
        [lax.dynamic_index_in_dim(value, place ^ step, keepdims=False) for step in range(count)], axis
    )
    return ordered(jnp.stack(parts), place)


def turn_exchange(parts):
    arrived = []
    for step, part in enumerate(parts):
        pairs = []
        for source in range(8):
            ey, ec, gh = source // 4, source // 2 % 2, source % 2
            pairs.append((source, (ey ^ (step // 2)) * 4 + gh * 2 + (ec ^ (step % 2))))
        arrived.append(lax.ppermute(part, ("ey", "ec", "gh"), pairs))
    return arrived


def in_order(own, other, axis, place=0):
    first = lax.axis_index(axis) == 0
    return jnp.stack([jnp.where(first, own, other), jnp.where(first, other, own)], axis=place)


def gather_pair(value, axis, place=0):
    return in_order(value, swap(value, axis), axis, place)


def gather_minor(value):
    if lax.axis_size("rs") == 1:
        return gather_pair(value, "ec")
    return lax.all_gather(value, MINOR)


def nearest_first(value):
    count = value.shape[0]
    return jnp.take(value, jnp.arange(count) ^ lax.axis_index(MINOR), axis=0, mode="clip")


def other_minor(value, columns):
    if lax.axis_size("rs") == 1:
        return swap(value, "ec")
    return nearest_first(lax.all_gather(value[:, :columns], MINOR))[1:].reshape(-1, columns)


def sum_nearest(own, low):
    if lax.axis_size("rs") == 1:
        return own + swap(low[0], "ec").astype(F32)
    parts = nearest_first(jnp.concatenate([own.astype(BF16)[None], low]))
    return jnp.sum(lax.all_to_all(parts, MINOR, 0, 0, tiled=True).astype(F32), axis=0)


def split_minor(parts):
    if lax.axis_size("rs") != 1:
        return (parts.astype(BF16),)
    first = lax.axis_index("ec") == 0
    sent = jnp.where(first, parts[1], parts[0]).astype(BF16)
    return (jnp.where(first, parts[0], parts[1]), sent)


def sum_split(split):
    if lax.axis_size("rs") != 1:
        arrived = lax.all_to_all(split[0], MINOR, 0, 0, tiled=True)
        return jnp.sum(arrived.astype(F32), axis=0)
    return split[0] + swap(split[1], "ec").astype(F32)


def swap_major(value):
    return lax.all_to_all(value, "mj", 0, 0, tiled=True)


def core_sum(value):
    value = value.reshape(lax.axis_size("ey"), 2, -1, value.shape[1])
    first = lax.axis_index("ec") == 0
    sent = jnp.where(first, value[:, 1], value[:, 0]).astype(BF16)
    value = jnp.where(first, value[:, 0], value[:, 1]) + swap(sent, "ec").astype(F32)
    return value.astype(BF16)


def scatter_rows(value):
    chips = math.prod(lax.axis_size(name) for name in REST)
    value = value.reshape(chips, -1, value.shape[-1])
    return lax.all_to_all(value, REST, 0, 0, tiled=True).astype(F32)


def after(value, *others):
    return lax.optimization_barrier((value, others))[0]


def unit(hidden):
    return lax.rsqrt(jnp.mean(hidden * hidden, axis=-1, keepdims=True) + EPS)


def per_device(
    activations,
    cotangent,
    query_key_weight,
    value_weight,
    output_weight,
    norm_first,
    norm_second,
    router_weight,
    bias_table,
    w_in,
    w_out,
    routes,
    slots,
):
    rows, width = activations.shape[1:]
    major = lax.axis_size("mj")
    rest = lax.axis_size("rs")
    minor = 2 * rest
    ring = 2 * major * rest
    experts = router_weight.shape[1]
    capacity = rows * 5 // (4 * experts)
    head_count = bias_table.shape[1]
    heads = head_count // major
    features = value_weight.shape[1]
    head_dim = features // head_count
    shard = query_key_weight.shape[0]
    my_major = lax.axis_index("mj")
    my_exp = lax.axis_index(("ey", "gh"))
    edges = bucket_edges(4 * rows)
    kv_width = heads * 2 * head_dim
    q_width = heads * head_dim
    extra_width = 128 - (kv_width + q_width) % 128
    packed_width = kv_width + q_width + extra_width

    numbers = jnp.concatenate([routes, slots]).astype(BF16)
    numbers = jnp.pad(numbers, ((0, 14), (0, width - rows)))
    both = jnp.concatenate([activations[0], numbers, w_out[:, 0, :]])
    query_key_weight, value_weight, w_in = after((query_key_weight, value_weight, w_in), both)
    both = turn(both)
    tokens = both[:rows]
    numbers = both[rows : rows + 2, :rows].astype(jnp.int32)
    outer = both[rows + 16 :]

    def by_head(value):
        return value.reshape(shard, major, heads, 1, head_dim)

    key_value = jnp.concatenate(
        [by_head(query_key_weight[:, features:]), by_head(value_weight)], axis=3
    ).reshape(shard, major, kv_width)
    extras = jnp.concatenate([router_weight, norm_first[:, None], norm_second[:, None]], axis=1)
    extras = jnp.pad(extras, ((0, 0), (0, extra_width - experts - 2)))
    packed = jnp.concatenate(
        [
            key_value,
            query_key_weight[:, :features].reshape(shard, major, q_width),
            jnp.broadcast_to(extras[:, None, :], (shard, major, extra_width)),
        ],
        axis=2,
    )
    packed = exchange_ordered(jnp.transpose(packed, (1, 0, 2)), "mj")
    background = packed
    if rest == 1:
        packed = jnp.stack([packed, swap(packed, "gh")])
        background = packed
        packed = jnp.concatenate([packed, swap(packed, "ey")])
        packed = ordered(packed, lax.axis_index(("ey", "gh"))).reshape(2, 2, major, shard, packed_width)
        packed = gather_pair(packed, "ec", 1)
    else:
        packed = lax.all_gather(packed, ("ey", "ec", "gh", "rs"))
        packed = packed.reshape(2, 2, 2, rest, major, shard, packed_width)
        packed = jnp.transpose(packed, (0, 1, 2, 4, 3, 5, 6))
    packed = packed.reshape(width, packed_width)
    extras = packed[:, kv_width + q_width :]
    full_router = extras[:, :experts]
    gain_first = extras[:, experts].astype(F32)
    gain_second = extras[:, experts + 1].astype(F32)

    column = jnp.stack(exchange([tokens] * major, "mj"))
    part = w_in.shape[2] // major
    half = part // 2
    inner = jnp.concatenate(
        [
            jnp.concatenate([w_in[:, 0, (side * major + i) * half :][:, :half] for side in range(2)], axis=1)
            for i in range(major)
        ]
    )
    inner = swap_major(inner.reshape(major, -1, part)).reshape(-1, part)
    inner = turn(after(jnp.concatenate([inner, cotangent[0]]), background))
    cotangent = after(cotangent[0], packed)

    full_o = lax.all_gather(output_weight, EVERY, axis=0, tiled=True)
    near_major = jnp.arange(major, dtype=jnp.int32) ^ my_major

    table = lax.dynamic_slice_in_dim(bias_table, my_major * heads, heads, axis=1).astype(F32)
    near = pl.pallas_call(
        functools.partial(near_bias_kernel, edges, rows),
        in_specs=[scalars()],
        out_shape=jax.ShapeDtypeStruct((heads, 3 * rows, rows), F32),
    )(table)
    far = jnp.stack([table[15], table[31]])
    near_minor = jnp.arange(minor, dtype=jnp.int32) ^ lax.axis_index(MINOR)
    key_blocks = (near_minor // rest)[:, None] * major + near_major[None, :]
    key_blocks = (key_blocks * rest + (near_minor % rest)[:, None]).reshape(-1)
    block_ids = jnp.arange(-1, ring + 1, dtype=jnp.int32)
    found = key_blocks[None, :] == block_ids[:, None]
    key_slots = jnp.where(found, jnp.arange(ring, dtype=jnp.int32)[None, :], 0)
    key_slots = jnp.where(jnp.any(found, axis=1), jnp.sum(key_slots, axis=1), ring)
    places = (key_blocks[:major], key_blocks, key_slots)

    expert_ids = jnp.arange(experts, dtype=jnp.int32)
    slot_ids = jnp.arange(capacity, dtype=jnp.int32)

    def selection(token_routes, token_slots, place):
        chosen = (
            ((token_routes ^ place)[None, None, :] == expert_ids[:, None, None])
            & (token_slots[None, None, :] == slot_ids[None, :, None])
        ).astype(BF16)
        return chosen.reshape(experts * capacity, rows)

    def by_expert(chosen, value):
        sent = dot_n(chosen, value).astype(BF16)
        return [sent[i * capacity : (i + 1) * capacity] for i in range(experts)]

    def gather_rows(parts):
        return exchange([jnp.concatenate(parts)] * major, "mj")

    def sum_parts(value):
        value = value.reshape(major, experts * capacity, width)
        return exchange([value[i] for i in range(major)], "mj")

    def send_back(parts):
        total = sum(part.astype(F32) for part in parts).astype(BF16)
        total = total.reshape(experts, capacity, width)
        return exchange([total[i] for i in range(experts)], ("ey", "gh"))

    sent = by_expert(selection(routes[0], slots[0], lax.axis_index(("ey", "ec"))), cotangent)
    cot_parts = turn_exchange(sent)
    routes, slots = numbers[0], numbers[1]
    select = selection(routes, slots, my_exp)

    column_hidden = column.reshape(major * rows, width).astype(F32)
    column_unit = unit(column_hidden)
    normed = (column_hidden * column_unit * gain_first).astype(BF16)
    projected = dot_n(normed, packed).astype(BF16)
    others = other_minor(projected, kv_width)
    outer = gather_minor(outer).reshape(part, width)
    attended_low, attended_wide, lse = forward_attention(
        projected, others, near, far, places, heads, rows
    )
    attended_low, cot_parts, inner, outer = lax.optimization_barrier(
        (attended_low, cot_parts, inner, outer)
    )
    my_cotangent = inner[-rows:]
    attended = exchange([attended_low[i * rows : (i + 1) * rows] for i in range(major)], "mj")
    attended = ordered(jnp.stack(attended), my_major)
    attended = jnp.transpose(attended, (1, 0, 2)).reshape(rows, features)

    hidden = tokens.astype(F32)
    middle = hidden + dot_n(attended, full_o)
    middle_unit = unit(middle)
    mixed = (middle * middle_unit * gain_second).astype(BF16)
    chances = jax.nn.softmax(dot_n(mixed, full_router), axis=-1)
    route_mask = (routes[:, None] == expert_ids[None, :]).astype(F32)
    gate = jnp.sum(chances * route_mask, axis=-1, keepdims=True)

    mixed_parts = exchange(by_expert(select, mixed), ("ey", "gh"))
    cot_rows = gather_rows(after(cot_parts, attended))
    inner = after(inner[:-rows], attended)
    inner = gather_minor(inner.reshape(major, -1, part)).reshape(2, rest, major, -1, part)
    inner = jnp.transpose(inner, (0, 2, 1, 3, 4)).reshape(width, part)
    buffer = gather_rows(mixed_parts)
    cot_rows = jnp.concatenate(after(cot_rows, mixed_parts))
    buffer = jnp.concatenate(lax.optimization_barrier(buffer))
    row_chances = jax.nn.softmax(dot_n(buffer, full_router), axis=-1)
    row_mask = (expert_ids == my_exp).astype(F32)[None, :]
    row_gate = jnp.sum(row_chances * row_mask, axis=-1, keepdims=True)
    preact = dot_n(buffer, inner)
    cumulative = 0.5 * (1.0 + lax.erf(preact * math.sqrt(0.5)))
    density = jnp.exp(-0.5 * preact * preact) * (1.0 / math.sqrt(2.0 * math.pi))
    activated_wide = preact * cumulative
    grad_activated = dot_t(cot_rows, outer)
    grad_preact = (row_gate * grad_activated * (cumulative + preact * density)).astype(BF16)
    row_grad_gate = jnp.sum(activated_wide * grad_activated, axis=-1, keepdims=True)
    grad_logits = (row_gate * row_grad_gate * (row_mask - row_chances)).astype(BF16)
    grad_mixed = dot_t(grad_preact, inner) + dot_t(grad_logits, full_router)
    grad_mixed = grad_mixed.astype(BF16)
    buffer, activated_wide, grad_preact, cot_rows = after(
        (buffer, activated_wide, grad_preact, cot_rows), grad_mixed
    )

    activated = activated_wide.astype(BF16)
    produced = dot_n(activated, outer).astype(BF16)
    grad_router = dot_0(buffer, grad_logits)
    gated_rows = (row_gate * cot_rows.astype(F32)).astype(BF16)
    grad_outer = dot_0(activated, gated_rows).reshape(minor, -1, width)
    grad_inner = dot_0(buffer, grad_preact).reshape(2, major, rest, -1, part)
    grad_inner = jnp.transpose(grad_inner, (0, 2, 1, 3, 4)).reshape(minor, -1, part)
    grad_outer, grad_inner, produced, grad_parts = lax.optimization_barrier(
        (split_minor(grad_outer), split_minor(grad_inner), produced, sum_parts(grad_mixed))
    )
    grad_parts = send_back(grad_parts)
    grad_outer = sum_split(grad_outer).astype(BF16)
    grad_inner = sum_split(grad_inner).astype(BF16).reshape(major, -1, part)
    grad_parts, grad_outer, grad_inner = lax.optimization_barrier((grad_parts, grad_outer, grad_inner))
    grad_mixed = dot_0(select, jnp.concatenate(grad_parts))
    grad_outer = turn(grad_outer)

    grad_z = my_cotangent.astype(F32)
    grad_gain_second = jnp.sum(grad_mixed * middle * middle_unit, axis=0)
    scaled = grad_mixed * gain_second
    grad_middle = (
        grad_z
        + middle_unit * scaled
        - middle * middle_unit**3 * jnp.mean(scaled * middle, axis=-1, keepdims=True)
    )
    grad_branch = grad_middle.astype(BF16)
    grad_attended = dot_t(grad_branch, full_o).astype(BF16)
    grad_attended = jnp.transpose(grad_attended.reshape(rows, major, q_width), (1, 0, 2))
    grad_attended = ordered(grad_attended, my_major)
    grad_attended = jnp.concatenate(exchange([grad_attended[i] for i in range(major)], "mj"))
    produced_parts = sum_parts(after(produced, grad_attended))
    grad_inner = swap_major(after(grad_inner, grad_mixed)).reshape(-1, part)
    grad_o = core_sum(dot_0(attended, grad_branch))

    dq, dkv, dkv_low, near_sum, far_sum = backward_attention(
        projected, grad_attended, attended_wide, others, near, far, places, lse, heads, rows
    )
    dq, dkv, dkv_low, grad_outer, grad_inner, produced_parts, grad_o = lax.optimization_barrier(
        (dq, dkv, dkv_low, grad_outer, grad_inner, produced_parts, grad_o)
    )
    grad_o = scatter_rows(grad_o)
    grad_inner = turn(grad_inner)
    dkv = sum_nearest(dkv, dkv_low.reshape(minor - 1, major * rows, kv_width)).astype(BF16)
    grad_projected = jnp.concatenate([dkv, dq], axis=1)
    grad_normed = dot_t(grad_projected, packed)
    parts = grad_normed.astype(BF16).reshape(major, rows, width)
    produced_parts, near_sum, normed, grad_projected = after(
        (produced_parts, near_sum, normed, grad_projected), parts
    )
    produced_parts = send_back(produced_parts)

    sums = pl.pallas_call(
        functools.partial(bucket_sum_kernel, edges, rows),
        out_shape=jax.ShapeDtypeStruct((heads, 128), F32),
    )(near_sum, far_sum)
    grad_table = sums[:, :32].T
    grad_gain_first = jnp.sum(grad_normed * column_hidden * column_unit, axis=0)
    grad_parts = exchange([parts[i] for i in range(major)], "mj")
    grad_parts, grad_inner, grad_outer = lax.optimization_barrier((grad_parts, grad_inner, grad_outer))
    grad_normed = sum(part.astype(F32) for part in grad_parts)
    produced = dot_0(select, jnp.concatenate(after(produced_parts, grad_normed)))
    layer_output = (middle + gate * produced).astype(BF16)
    hidden_unit = unit(hidden)
    scaled = grad_normed * gain_first
    grad_activations = (
        grad_middle
        + hidden_unit * scaled
        - hidden * hidden_unit**3 * jnp.mean(scaled * hidden, axis=-1, keepdims=True)
    ).astype(BF16)
    both = turn(jnp.concatenate([grad_activations, layer_output]))
    grad_activations, layer_output = both[None, :rows], both[None, rows:]

    buckets = bias_table.shape[0]
    table_columns = buckets * heads // shard
    flat_table = jnp.tile(
        grad_table.reshape(shard, table_columns), (width // shard, 1)
    )
    small = jnp.concatenate(
        [grad_router, grad_gain_first[:, None], grad_gain_second[:, None], flat_table], axis=1
    )
    small = jnp.pad(small, ((0, 0), (kv_width + q_width, extra_width - small.shape[1])))
    arrived = scatter_rows(core_sum(dot_0(normed, grad_projected) + small))
    arrived = arrived.reshape(4, major, rest, shard, packed_width)
    arrived = jnp.sum(arrived, axis=(0, 2))
    key_value = arrived[:, :, :kv_width].reshape(major, shard, heads, 2, head_dim)

    def side_by_side(value):
        return jnp.transpose(value.reshape(major, shard, q_width), (1, 0, 2)).reshape(shard, features)

    grad_query = side_by_side(arrived[:, :, kv_width : kv_width + q_width])
    grad_key = side_by_side(key_value[:, :, :, 0, :])
    grad_v = side_by_side(key_value[:, :, :, 1, :])
    small = arrived[:, :, kv_width + q_width :]
    summed = jnp.sum(small[:, :, : experts + 2], axis=0)
    grad_table = small[:, :, experts + 2 : experts + 2 + table_columns]
    grad_table = jnp.transpose(grad_table.reshape(major, buckets, heads), (1, 0, 2))
    grad_o = jnp.sum(grad_o, axis=0)
    grad_inner = unpack(grad_inner.reshape(major, w_in.shape[0], part), 2)
    grad_outer = unpack(grad_outer[None], 1)
    return (
        layer_output,
        grad_activations,
        jnp.concatenate([grad_query, grad_key], axis=1),
        grad_v,
        grad_o,
        summed[:, experts],
        summed[:, experts + 1],
        summed[:, :experts],
        grad_table.reshape(buckets, head_count),
        grad_inner,
        grad_outer,
    )


def solution(mesh):
    groups, ring = mesh.shape["exp"], mesh.shape["ctx"]
    split = Mesh(mesh.devices.reshape(groups // 2, 2, 2, 4, ring // 8), EVERY)
    exp, ctx = ("ey", "ec"), ("gh", "mj", "rs")
    tokens, rows, experts = P(exp, ctx, None), P(EVERY, None), P(ctx, exp, None)
    return jax.shard_map(
        per_device,
        mesh=split,
        in_specs=(
            tokens,
            tokens,
            rows,
            rows,
            rows,
            P(EVERY),
            P(EVERY),
            rows,
            P(),
            experts,
            experts,
            P(exp, ctx),
            P(exp, ctx),
        ),
        out_specs=(
            tokens,
            tokens,
            rows,
            rows,
            rows,
            P(EVERY),
            P(EVERY),
            rows,
            P(),
            experts,
            experts,
        ),
        check_vma=False,
    )
```

```python
import functools
import math

import jax
import jax.numpy as jnp
import numpy as np
from jax import lax
from jax.experimental import pallas as pl
from jax.experimental.pallas import tpu as pltpu
from jax.sharding import Mesh
from jax.sharding import PartitionSpec as P

EPS = 1e-06
F32 = jnp.float32
BF16 = jnp.bfloat16
EVERY = ("ey", "ec", "gh", "mj", "rs")
MINOR = ("ec", "rs")
REST = ("ey", "gh", "mj", "rs")
VMEM_BYTES = 56 * 1024 * 1024


def bucket_edges(reach):
    magnitude = np.arange(reach)
    spread = 8 + (np.log(np.maximum(magnitude, 1) / 8.0) / np.log(16.0) * 8.0).astype(np.int64)
    bucket = np.where(magnitude < 8, magnitude, np.minimum(spread, 15))
    return [int(np.argmax(bucket >= number)) for number in range(16)]


def dot_t(left, right):
    return lax.dot_general(left, right, (((1,), (1,)), ((), ())), preferred_element_type=F32)


def dot_0(left, right):
    return lax.dot_general(left, right, (((0,), (0,)), ((), ())), preferred_element_type=F32)


def dot_n(left, right):
    return jnp.dot(left, right, preferred_element_type=F32)


def near_bias_kernel(edges, rows, table_ref, out_ref):
    shape = (3 * rows, rows)
    relative = (
        lax.broadcasted_iota(jnp.int32, shape, 0) - rows - lax.broadcasted_iota(jnp.int32, shape, 1)
    )
    magnitude = jnp.abs(relative)
    ahead = relative > 0
    for head in range(out_ref.shape[0]):
        value = jnp.where(ahead, table_ref[16, head], table_ref[0, head])
        for number in range(1, 16):
            value = jnp.where(
                magnitude >= edges[number],
                jnp.where(ahead, table_ref[16 + number, head], table_ref[number, head]),
                value,
            )
        out_ref[head] = value


def bucket_sum_kernel(edges, rows, near_ref, far_ref, out_ref):
    shape = (3 * rows, rows)
    relative = (
        lax.broadcasted_iota(jnp.int32, shape, 0) - rows - lax.broadcasted_iota(jnp.int32, shape, 1)
    )
    magnitude = jnp.abs(relative)
    lanes = lax.broadcasted_iota(jnp.int32, (1, 128), 1)
    for head in range(near_ref.shape[0]):
        grads = near_ref[head]
        behind = jnp.where(relative > 0, 0.0, grads)
        forward = jnp.where(relative > 0, grads, 0.0)
        total = jnp.zeros((1, 128), F32)
        for side, part in enumerate((behind, forward)):
            for number in range(16):
                inside = magnitude >= edges[number]
                if number < 15:
                    inside = inside & (magnitude < edges[number + 1])
                value = jnp.sum(jnp.sum(jnp.where(inside, part, 0.0), axis=0, keepdims=True))
                if number == 15:
                    value = value + jnp.sum(far_ref[head, side : side + 1, :])
                total = jnp.where(lanes == side * 16 + number, value, total)
        out_ref[head : head + 1, :] = total


def biased_scores(parts, key_ref, place_ref, far_ref, near_ref, scratch, head, block, rows):
    pieces = [
        part[first : first + rows, :] for part in parts for first in range(0, part.shape[0], rows)
    ]
    slots = len(pieces)
    for slot in range(slots):
        far = jnp.where(
            key_ref[slot] < block - 1,
            far_ref[0, head],
            jnp.where(key_ref[slot] > block + 1, far_ref[1, head], 0.0),
        )
        scratch[slot * rows : (slot + 1) * rows, :] = pieces[slot] + far
    for step in range(3):
        window = pl.ds(pl.multiple_of(place_ref[block + step] * rows, rows), rows)
        scratch[window, :] = scratch[window, :] + near_ref[head, step * rows : (step + 1) * rows, :]
    return scratch[0 : slots * rows, :]


def head_queries(q_ref, heads, head):
    first = heads * 128 + head * 64
    query = q_ref[:, first : first + 64]
    return jnp.concatenate([query, jnp.zeros_like(query)], axis=1)


def attention_kernel(
    heads,
    rows,
    block_ref,
    key_ref,
    place_ref,
    far_ref,
    q_ref,
    own_ref,
    other_ref,
    near_ref,
    low_ref,
    wide_ref,
    lse_ref,
    scratch,
):
    block = block_ref[pl.program_id(0)]
    own_rows = own_ref.shape[0]
    for head in range(heads):
        lanes = slice(head * 128, (head + 1) * 128)
        own, other = own_ref[:, lanes], other_ref[:, lanes]
        query = head_queries(q_ref, heads, head)
        scores = biased_scores(
            (dot_t(own, query), dot_t(other, query)),
            key_ref,
            place_ref,
            far_ref,
            near_ref,
            scratch.at[head % scratch.shape[0]],
            head,
            block,
            rows,
        )
        top = jnp.max(scores, axis=0, keepdims=True)
        weights = jnp.exp(scores - top)
        total = jnp.sum(weights, axis=0, keepdims=True)
        low = (weights * (1.0 / total)).astype(BF16)
        result = dot_0(low[:own_rows], own) + dot_0(low[own_rows:], other)
        wide_ref[:, lanes] = result
        low_ref[:, head * 64 : (head + 1) * 64] = result[:, 64:].astype(BF16)
        lse_ref[0, head : head + 1, :] = top + jnp.log(total)


def attention_back_kernel(
    heads,
    rows,
    block_ref,
    key_ref,
    place_ref,
    far_ref,
    q_ref,
    g_ref,
    wide_ref,
    own_ref,
    other_ref,
    near_ref,
    lse_ref,
    dq_ref,
    sum_ref,
    low_ref,
    near_sum_ref,
    far_sum_ref,
    scratch,
    grad_scratch,
    total_scratch,
):
    step = pl.program_id(0)
    block = block_ref[step]
    own_rows = own_ref.shape[0]
    count = own_rows + other_ref.shape[0]
    slots = count // rows

    @pl.when(step == 0)
    def _():
        total_scratch[...] = jnp.zeros_like(total_scratch)
        near_sum_ref[...] = jnp.zeros_like(near_sum_ref)
        far_sum_ref[...] = jnp.zeros_like(far_sum_ref)
        for copy in range(grad_scratch.shape[0]):
            grad_scratch[copy, count : count + rows, :] = jnp.zeros((rows, rows), F32)

    for head in range(heads):
        copy = head % scratch.shape[0]
        lanes = slice(head * 128, (head + 1) * 128)
        own, other = own_ref[:, lanes], other_ref[:, lanes]
        grad = g_ref[:, head * 64 : (head + 1) * 64]
        grad = jnp.concatenate([jnp.zeros_like(grad), grad], axis=1)
        delta = jnp.sum(jnp.transpose(grad.astype(F32) * wide_ref[:, lanes]), axis=0, keepdims=True)
        both = jnp.concatenate([head_queries(q_ref, heads, head), grad], axis=0)
        first, second = dot_t(own, both), dot_t(other, both)
        scores = biased_scores(
            (first[:, :rows], second[:, :rows]),
            key_ref,
            place_ref,
            far_ref,
            near_ref,
            scratch.at[copy],
            head,
            block,
            rows,
        )
        chances = jnp.exp(scores - lse_ref[0, head : head + 1, :])
        products = jnp.concatenate([first[:, rows:], second[:, rows:]], axis=0)
        grads = chances * (products - delta)
        grads_low = grads.astype(BF16)
        grad_scratch[copy, 0:count, :] = grads
        for part in range(3):
            window = pl.ds(pl.multiple_of(place_ref[block + part] * rows, rows), rows)
            near_sum_ref[head, part * rows : (part + 1) * rows, :] += grad_scratch[copy, window, :]
        low_far = jnp.zeros((1, rows), F32)
        high_far = jnp.zeros((1, rows), F32)
        for slot in range(slots):
            line = jnp.sum(grads[slot * rows : (slot + 1) * rows, :], axis=0, keepdims=True)
            low_far = low_far + line * jnp.where(key_ref[slot] < block - 1, 1.0, 0.0)
            high_far = high_far + line * jnp.where(key_ref[slot] > block + 1, 1.0, 0.0)
        far_sum_ref[head, 0:1, :] += low_far
        far_sum_ref[head, 1:2, :] += high_far
        pair = jnp.concatenate([grads_low, chances.astype(BF16)], axis=1)
        total_scratch[:, lanes] += dot_n(pair, both)
        dq = dot_0(grads_low[:own_rows], own) + dot_0(grads_low[own_rows:], other)
        dq_ref[:, head * 64 : (head + 1) * 64] = dq[:, :64].astype(BF16)

    dq_ref[:, heads * 64 :] = jnp.zeros_like(dq_ref[:, heads * 64 :])

    @pl.when(step == pl.num_programs(0) - 1)
    def _():
        sum_ref[...] = total_scratch[0:own_rows, :]
        low_ref[...] = total_scratch[own_rows:count, :].astype(BF16)


def column_kernel(major, heads, size, in_ref, qk_ref, v_ref, small_ref):
    terms = in_ref.shape[0] // major
    for group in range(major):
        total = in_ref[group].astype(F32)
        for term in range(1, terms):
            total = total + in_ref[term * major + group].astype(F32)
        queries, start = heads * 2 * size, group * heads * size
        features = major * heads * size
        qk_ref[:, start : start + heads * size] = total[:, queries : queries + heads * size]
        for head in range(heads):
            first, place = head * 2 * size, start + head * size
            qk_ref[:, features + place : features + place + size] = total[:, first : first + size]
            v_ref[:, place : place + size] = total[:, first + size : first + 2 * size]
        small_ref[group] = total[:, queries + heads * size :]


def split_columns(value, major, heads, size):
    rows, columns = value.shape[1:]
    features = major * heads * size
    return pl.pallas_call(
        functools.partial(column_kernel, major, heads, size),
        out_shape=[
            jax.ShapeDtypeStruct((rows, 2 * features), F32),
            jax.ShapeDtypeStruct((rows, features), F32),
            jax.ShapeDtypeStruct((major, rows, columns - 3 * heads * size), F32),
        ],
    )(value)


def unpack_kernel(cuts, in_ref, out_ref):
    count = in_ref.shape[0]
    step = in_ref.shape[2] // cuts
    for cut in range(cuts):
        for index in range(count):
            first = (cut * count + index) * step
            value = in_ref[index, :, cut * step : (cut + 1) * step].astype(F32)
            out_ref[:, 0, first : first + step] = value


def unpack(value, cuts):
    count, rows, columns = value.shape
    return pl.pallas_call(
        functools.partial(unpack_kernel, cuts),
        out_shape=jax.ShapeDtypeStruct((rows, 1, count * columns), F32),
    )(value)


def whole_block(shape):
    zeros = (0,) * len(shape)
    return pl.BlockSpec(shape, lambda *_: zeros)


def scalars():
    return pl.BlockSpec(memory_space=pltpu.SMEM)


def slot_count(heads, count):
    return heads if count <= 2048 else 1


def estimate(products, steps, rows, count, heads):
    return pl.CostEstimate(
        flops=2 * products * steps * rows * count * heads * 128,
        bytes_accessed=1024 * count * heads,
        transcendentals=steps * rows * count * heads,
    )


def forward_attention(projected, other, near, far, places, heads, rows):
    steps = places[0].shape[0]
    own = steps * rows
    count = own + other.shape[0]
    width = heads * 128
    return pl.pallas_call(
        functools.partial(attention_kernel, heads, rows),
        grid=(steps,),
        in_specs=[scalars()] * 4
        + [
            pl.BlockSpec((rows, projected.shape[1]), lambda i: (i, 0)),
            whole_block((own, width)),
            whole_block((count - own, width)),
            whole_block(near.shape),
        ],
        out_specs=[
            pl.BlockSpec((rows, width // 2), lambda i: (i, 0)),
            pl.BlockSpec((rows, width), lambda i: (i, 0)),
            pl.BlockSpec((1, heads, rows), lambda i: (i, 0, 0)),
        ],
        out_shape=[
            jax.ShapeDtypeStruct((own, width // 2), BF16),
            jax.ShapeDtypeStruct((own, width), F32),
            jax.ShapeDtypeStruct((steps, heads, rows), F32),
        ],
        scratch_shapes=[pltpu.VMEM((slot_count(heads, count), count + rows, rows), F32)],
        compiler_params=pltpu.CompilerParams(vmem_limit_bytes=VMEM_BYTES),
        cost_estimate=estimate(2, steps, rows, count, heads),
    )(*places, far, projected, projected, other, near)


def backward_attention(projected, grads, wide, other, near, far, places, lse, heads, rows):
    steps = places[0].shape[0]
    own = steps * rows
    count = own + other.shape[0]
    width = heads * 128
    dq_width = -(-width // 256) * 128
    slots = slot_count(heads, count)
    return pl.pallas_call(
        functools.partial(attention_back_kernel, heads, rows),
        grid=(steps,),
        in_specs=[scalars()] * 4
        + [
            pl.BlockSpec((rows, projected.shape[1]), lambda i: (i, 0)),
            pl.BlockSpec((rows, width // 2), lambda i: (i, 0)),
            pl.BlockSpec((rows, width), lambda i: (i, 0)),
            whole_block((own, width)),
            whole_block((count - own, width)),
            whole_block(near.shape),
            pl.BlockSpec((1, heads, rows), lambda i: (i, 0, 0)),
        ],
        out_specs=[
            pl.BlockSpec((rows, dq_width), lambda i: (i, 0)),
            whole_block((own, width)),
            whole_block((count - own, width)),
            whole_block(near.shape),
            whole_block((heads, 2, rows)),
        ],
        out_shape=[
            jax.ShapeDtypeStruct((own, dq_width), BF16),
            jax.ShapeDtypeStruct((own, width), F32),
            jax.ShapeDtypeStruct((count - own, width), BF16),
            jax.ShapeDtypeStruct(near.shape, F32),
            jax.ShapeDtypeStruct((heads, 2, rows), F32),
        ],
        scratch_shapes=[
            pltpu.VMEM((slots, count + rows, rows), F32),
            pltpu.VMEM((slots, count + rows, rows), F32),
            pltpu.VMEM((count, width), F32),
        ],
        compiler_params=pltpu.CompilerParams(vmem_limit_bytes=VMEM_BYTES),
        cost_estimate=estimate(5, steps, rows, count, heads),
    )(*places, far, projected, grads, wide, projected, other, near, lse)


def swap(value, axis):
    return lax.ppermute(value, axis, [(0, 1), (1, 0)])


def turn(value):
    return lax.ppermute(value, ("ec", "gh"), [(0, 0), (1, 2), (2, 1), (3, 3)])


def exchange(parts, axis):
    count = len(parts)
    return [parts[0]] + [
        lax.ppermute(parts[step], axis, [(source, source ^ step) for source in range(count)])
        for step in range(1, count)
    ]


def ordered(value, place):
    count = value.shape[0]
    return jnp.take(value, jnp.arange(count) ^ place, axis=0, mode="clip")


def exchange_ordered(value, axis):
    place = lax.axis_index(axis)
    count = value.shape[0]
    parts = exchange(
        [lax.dynamic_index_in_dim(value, place ^ step, keepdims=False) for step in range(count)], axis
    )
    return ordered(jnp.stack(parts), place)


def turn_exchange(parts):
    arrived = []
    for step, part in enumerate(parts):
        pairs = []
        for source in range(8):
            ey, ec, gh = source // 4, source // 2 % 2, source % 2
            pairs.append((source, (ey ^ (step // 2)) * 4 + gh * 2 + (ec ^ (step % 2))))
        arrived.append(lax.ppermute(part, ("ey", "ec", "gh"), pairs))
    return arrived


def in_order(own, other, axis, place=0):
    first = lax.axis_index(axis) == 0
    return jnp.stack([jnp.where(first, own, other), jnp.where(first, other, own)], axis=place)


def gather_pair(value, axis, place=0):
    return in_order(value, swap(value, axis), axis, place)


def gather_minor(value):
    if lax.axis_size("rs") == 1:
        return gather_pair(value, "ec")
    return lax.all_gather(value, MINOR)


def nearest_first(value):
    count = value.shape[0]
    return jnp.take(value, jnp.arange(count) ^ lax.axis_index(MINOR), axis=0, mode="clip")


def other_minor(value, columns):
    if lax.axis_size("rs") == 1:
        return swap(value, "ec")
    return nearest_first(lax.all_gather(value[:, :columns], MINOR))[1:].reshape(-1, columns)


def sum_nearest(own, low):
    if lax.axis_size("rs") == 1:
        return own + swap(low[0], "ec").astype(F32)
    parts = nearest_first(jnp.concatenate([own.astype(BF16)[None], low]))
    return jnp.sum(lax.all_to_all(parts, MINOR, 0, 0, tiled=True).astype(F32), axis=0)


def split_minor(parts):
    if lax.axis_size("rs") != 1:
        return (parts.astype(BF16),)
    first = lax.axis_index("ec") == 0
    sent = jnp.where(first, parts[1], parts[0]).astype(BF16)
    return (jnp.where(first, parts[0], parts[1]), sent)


def sum_split(split):
    if lax.axis_size("rs") != 1:
        arrived = lax.all_to_all(split[0], MINOR, 0, 0, tiled=True)
        return jnp.sum(arrived.astype(F32), axis=0)
    return split[0] + swap(split[1], "ec").astype(F32)


def swap_major(value):
    return lax.all_to_all(value, "mj", 0, 0, tiled=True)


def core_sum(value):
    value = value.reshape(lax.axis_size("ey"), 2, -1, value.shape[1])
    first = lax.axis_index("ec") == 0
    sent = jnp.where(first, value[:, 1], value[:, 0]).astype(BF16)
    value = jnp.where(first, value[:, 0], value[:, 1]) + swap(sent, "ec").astype(F32)
    return value.astype(BF16)


def scatter_rows(value):
    chips = math.prod(lax.axis_size(name) for name in REST)
    value = value.reshape(chips, -1, value.shape[-1])
    return lax.all_to_all(value, REST, 0, 0, tiled=True)


def after(value, *others):
    return lax.optimization_barrier((value, others))[0]


def unit(hidden):
    return lax.rsqrt(jnp.mean(hidden * hidden, axis=-1, keepdims=True) + EPS)


def per_device(
    activations,
    cotangent,
    query_key_weight,
    value_weight,
    output_weight,
    norm_first,
    norm_second,
    router_weight,
    bias_table,
    w_in,
    w_out,
    routes,
    slots,
):
    rows, width = activations.shape[1:]
    major = lax.axis_size("mj")
    rest = lax.axis_size("rs")
    minor = 2 * rest
    ring = 2 * major * rest
    experts = router_weight.shape[1]
    capacity = rows * 5 // (4 * experts)
    head_count = bias_table.shape[1]
    heads = head_count // major
    features = value_weight.shape[1]
    head_dim = features // head_count
    shard = query_key_weight.shape[0]
    my_major = lax.axis_index("mj")
    my_exp = lax.axis_index(("ey", "gh"))
    edges = bucket_edges(4 * rows)
    kv_width = heads * 2 * head_dim
    q_width = heads * head_dim
    extra_width = 128 - (kv_width + q_width) % 128
    packed_width = kv_width + q_width + extra_width

    numbers = jnp.concatenate([routes, slots]).astype(BF16)
    numbers = jnp.pad(numbers, ((0, 14), (0, width - rows)))
    both = jnp.concatenate([activations[0], numbers])
    query_key_weight, value_weight, w_in = after((query_key_weight, value_weight, w_in), both)
    both = turn(both)
    tokens = both[:rows]
    numbers = both[rows : rows + 2, :rows].astype(jnp.int32)

    def by_head(value):
        return value.reshape(shard, major, heads, 1, head_dim)

    key_value = jnp.concatenate(
        [by_head(query_key_weight[:, features:]), by_head(value_weight)], axis=3
    ).reshape(shard, major, kv_width)
    extras = jnp.concatenate([router_weight, norm_first[:, None], norm_second[:, None]], axis=1)
    extras = jnp.pad(extras, ((0, 0), (0, extra_width - experts - 2)))
    packed = jnp.concatenate(
        [
            key_value,
            query_key_weight[:, :features].reshape(shard, major, q_width),
            jnp.broadcast_to(extras[:, None, :], (shard, major, extra_width)),
        ],
        axis=2,
    )
    packed = exchange_ordered(jnp.transpose(packed, (1, 0, 2)), "mj")
    column = exchange([tokens] * major, "mj")

    expert_ids = jnp.arange(experts, dtype=jnp.int32)
    slot_ids = jnp.arange(capacity, dtype=jnp.int32)

    def selection(token_routes, token_slots, place):
        chosen = (
            ((token_routes ^ place)[None, None, :] == expert_ids[:, None, None])
            & (token_slots[None, None, :] == slot_ids[None, :, None])
        ).astype(BF16)
        return chosen.reshape(experts * capacity, rows)

    def by_expert(chosen, value):
        sent = dot_n(chosen, value).astype(BF16)
        return [sent[i * capacity : (i + 1) * capacity] for i in range(experts)]

    sent = by_expert(selection(routes[0], slots[0], lax.axis_index(("ey", "ec"))), cotangent[0])
    cot_parts = turn_exchange(after(sent, packed))
    routes, slots = numbers[0], numbers[1]
    select = selection(routes, slots, my_exp)

    background = packed
    if rest == 1:
        packed = jnp.stack([packed, swap(packed, "gh")])
        background = packed
        packed = jnp.concatenate([packed, swap(packed, "ey")])
        packed, column, cot_parts = lax.optimization_barrier((packed, column, cot_parts))
        packed = ordered(packed, lax.axis_index(("ey", "gh"))).reshape(2, 2, major, shard, packed_width)
        packed = gather_pair(packed, "ec", 1)
    else:
        packed = lax.all_gather(packed, ("ey", "ec", "gh", "rs"))
        packed = packed.reshape(2, 2, 2, rest, major, shard, packed_width)
        packed = jnp.transpose(packed, (0, 1, 2, 4, 3, 5, 6))
    packed = packed.reshape(width, packed_width)
    extras = packed[:, kv_width + q_width :]
    full_router = extras[:, :experts]
    gain_first = extras[:, experts].astype(F32)
    gain_second = extras[:, experts + 1].astype(F32)

    column = jnp.stack(column)
    part = w_in.shape[2] // major
    half = part // 2
    inner = jnp.concatenate(
        [
            jnp.concatenate([w_in[:, 0, (side * major + i) * half :][:, :half] for side in range(2)], axis=1)
            for i in range(major)
        ]
    )
    inner = swap_major(inner.reshape(major, -1, part)).reshape(-1, part)
    both = jnp.concatenate([inner, w_out[:, 0, :], cotangent[0]])
    both = turn(after(both, background))

    full_o = lax.all_gather(output_weight, EVERY, axis=0, tiled=True)
    near_major = jnp.arange(major, dtype=jnp.int32) ^ my_major

    table = lax.dynamic_slice_in_dim(bias_table, my_major * heads, heads, axis=1).astype(F32)
    near = pl.pallas_call(
        functools.partial(near_bias_kernel, edges, rows),
        in_specs=[scalars()],
        out_shape=jax.ShapeDtypeStruct((heads, 3 * rows, rows), F32),
    )(table)
    far = jnp.stack([table[15], table[31]])
    near_minor = jnp.arange(minor, dtype=jnp.int32) ^ lax.axis_index(MINOR)
    key_blocks = (near_minor // rest)[:, None] * major + near_major[None, :]
    key_blocks = (key_blocks * rest + (near_minor % rest)[:, None]).reshape(-1)
    block_ids = jnp.arange(-1, ring + 1, dtype=jnp.int32)
    found = key_blocks[None, :] == block_ids[:, None]
    key_slots = jnp.where(found, jnp.arange(ring, dtype=jnp.int32)[None, :], 0)
    key_slots = jnp.where(jnp.any(found, axis=1), jnp.sum(key_slots, axis=1), ring)
    places = (key_blocks[:major], key_blocks, key_slots)

    def gather_rows(parts):
        return exchange([jnp.concatenate(parts)] * major, "mj")

    def in_parts(value):
        count = experts * capacity
        return [value[i * count : (i + 1) * count] for i in range(major)]

    def send_back(parts):
        total = sum(part.astype(F32) for part in parts).astype(BF16)
        total = total.reshape(experts, capacity, width)
        return exchange([total[i] for i in range(experts)], ("ey", "gh"))

    cot_rows = gather_rows(cot_parts)

    column_hidden = column.reshape(major * rows, width).astype(F32)
    column_unit = unit(column_hidden)
    normed = (column_hidden * column_unit * gain_first).astype(BF16)
    projected = dot_n(normed, packed).astype(BF16)
    others = other_minor(projected, kv_width)
    attended_low, attended_wide, lse = forward_attention(
        projected, others, near, far, places, heads, rows
    )
    attended_low, cot_rows = lax.optimization_barrier((attended_low, cot_rows))
    attended = exchange([attended_low[i * rows : (i + 1) * rows] for i in range(major)], "mj")
    attended = lax.optimization_barrier(attended)
    attended = lax.optimization_barrier(ordered(jnp.stack(attended), my_major))
    attended = jnp.concatenate([attended[i] for i in range(major)], axis=1)

    hidden = tokens.astype(F32)
    middle = hidden + dot_n(attended, full_o)
    middle_unit = unit(middle)
    mixed = (middle * middle_unit * gain_second).astype(BF16)
    chances = jax.nn.softmax(dot_n(mixed, full_router), axis=-1)
    route_mask = (routes[:, None] == expert_ids[None, :]).astype(F32)
    gate = jnp.sum(chances * route_mask, axis=-1, keepdims=True)
    mixed_parts = exchange(by_expert(select, mixed), ("ey", "gh"))
    both = after(both, attended)
    my_cotangent = both[-rows:]
    inner = both[: major * w_in.shape[0]]
    outer = gather_minor(both[major * w_in.shape[0] : -rows]).reshape(part, width)
    inner = gather_minor(inner.reshape(major, -1, part)).reshape(2, rest, major, -1, part)
    inner = jnp.transpose(inner, (0, 2, 1, 3, 4)).reshape(width, part)
    buffer = gather_rows(mixed_parts)
    cot_rows = jnp.concatenate(after(cot_rows, mixed_parts))
    buffer = jnp.concatenate(lax.optimization_barrier(buffer))
    row_chances = jax.nn.softmax(dot_n(buffer, full_router), axis=-1)
    row_mask = (expert_ids == my_exp).astype(F32)[None, :]
    row_gate = jnp.sum(row_chances * row_mask, axis=-1, keepdims=True)
    preact = dot_n(buffer, inner)
    cumulative = 0.5 * (1.0 + lax.erf(preact * math.sqrt(0.5)))
    density = jnp.exp(-0.5 * preact * preact) * (1.0 / math.sqrt(2.0 * math.pi))
    activated_wide = preact * cumulative
    grad_activated = dot_t(cot_rows, outer)
    grad_preact = (row_gate * grad_activated * (cumulative + preact * density)).astype(BF16)
    row_grad_gate = jnp.sum(activated_wide * grad_activated, axis=-1, keepdims=True)
    grad_logits = (row_gate * row_grad_gate * (row_mask - row_chances)).astype(BF16)
    grad_mixed = dot_t(grad_preact, inner) + dot_t(grad_logits, full_router)
    grad_mixed = grad_mixed.astype(BF16)
    buffer, activated_wide, grad_preact, cot_rows = after(
        (buffer, activated_wide, grad_preact, cot_rows), grad_mixed
    )

    activated = activated_wide.astype(BF16)
    produced = dot_n(activated, outer).astype(BF16)
    produced = in_parts(produced)
    grad_router = dot_0(buffer, grad_logits)
    gated_rows = (row_gate * cot_rows.astype(F32)).astype(BF16)
    grad_outer = dot_0(activated, gated_rows).reshape(minor, -1, width)
    grad_inner = dot_0(buffer, grad_preact).reshape(2, major, rest, -1, part)
    grad_inner = jnp.transpose(grad_inner, (0, 2, 1, 3, 4)).reshape(minor, -1, part)
    grad_outer, grad_inner, produced, grad_parts = lax.optimization_barrier(
        (split_minor(grad_outer), split_minor(grad_inner), produced, exchange(in_parts(grad_mixed), "mj"))
    )
    grad_parts = send_back(grad_parts)
    produced_parts = exchange(produced, "mj")
    grad_outer = sum_split(grad_outer).astype(BF16)
    grad_inner = sum_split(grad_inner).astype(BF16).reshape(major, -1, part)
    grad_parts, grad_outer, grad_inner = lax.optimization_barrier((grad_parts, grad_outer, grad_inner))
    grad_mixed = dot_0(select, jnp.concatenate(grad_parts))

    grad_z = my_cotangent.astype(F32)
    grad_gain_second = jnp.sum(grad_mixed * middle * middle_unit, axis=0)
    scaled = grad_mixed * gain_second
    grad_middle = (
        grad_z
        + middle_unit * scaled
        - middle * middle_unit**3 * jnp.mean(scaled * middle, axis=-1, keepdims=True)
    )
    grad_branch = grad_middle.astype(BF16)
    grad_attended = [
        dot_t(
            grad_branch, lax.dynamic_slice_in_dim(full_o, (my_major ^ i) * q_width, q_width)
        ).astype(BF16)
        for i in range(major)
    ]
    grad_inner, grad_outer, attended, grad_branch = after(
        (grad_inner, grad_outer, attended, grad_branch), grad_attended
    )
    grad_attended = exchange(grad_attended, "mj")
    grad_attended = jnp.concatenate(lax.optimization_barrier(grad_attended))
    grad_outer = turn(grad_outer)
    grad_inner = swap_major(grad_inner).reshape(-1, part)
    grad_o = core_sum(dot_0(attended, grad_branch))

    dq, dkv, dkv_low, near_sum, far_sum = backward_attention(
        projected, grad_attended, attended_wide, others, near, far, places, lse, heads, rows
    )
    dq, dkv, dkv_low, grad_inner = lax.optimization_barrier((dq, dkv, dkv_low, grad_inner))
    grad_inner = turn(grad_inner)
    dkv = sum_nearest(dkv, dkv_low.reshape(minor - 1, major * rows, kv_width)).astype(BF16)
    grad_projected = jnp.concatenate([dkv, dq], axis=1)
    grad_normed = dot_t(grad_projected, packed)
    parts = grad_normed.astype(BF16).reshape(major, rows, width)
    produced_parts, near_sum, normed, grad_projected, grad_o, grad_outer = after(
        (produced_parts, near_sum, normed, grad_projected, grad_o, grad_outer), parts
    )
    produced_parts = send_back(produced_parts)
    grad_o = scatter_rows(grad_o)

    sums = pl.pallas_call(
        functools.partial(bucket_sum_kernel, edges, rows),
        out_shape=jax.ShapeDtypeStruct((heads, 128), F32),
    )(near_sum, far_sum)
    grad_table = sums[:, :32].T
    grad_gain_first = jnp.sum(grad_normed * column_hidden * column_unit, axis=0)
    grad_parts = exchange([parts[i] for i in range(major)], "mj")
    grad_outer = unpack(grad_outer[None], 1)
    grad_parts, grad_outer = lax.optimization_barrier((grad_parts, grad_outer))
    grad_normed = sum(part.astype(F32) for part in grad_parts)
    buckets = bias_table.shape[0]
    table_columns = buckets * heads // shard
    flat_table = jnp.tile(
        grad_table.reshape(shard, table_columns), (width // shard, 1)
    )
    small = jnp.concatenate(
        [grad_router, grad_gain_first[:, None], grad_gain_second[:, None], flat_table], axis=1
    )
    small = jnp.pad(small, ((0, 0), (kv_width + q_width, extra_width - small.shape[1])))
    grad_weight = core_sum(dot_0(normed, grad_projected) + small)
    produced = dot_0(select, jnp.concatenate(after(produced_parts, grad_normed, grad_weight)))
    layer_output = (middle + gate * produced).astype(BF16)
    hidden_unit = unit(hidden)
    scaled = grad_normed * gain_first
    grad_activations = (
        grad_middle
        + hidden_unit * scaled
        - hidden * hidden_unit**3 * jnp.mean(scaled * hidden, axis=-1, keepdims=True)
    ).astype(BF16)
    both = turn(jnp.concatenate([grad_activations, layer_output]))
    arrived = scatter_rows(grad_weight)
    grad_inner = unpack(grad_inner.reshape(major, w_in.shape[0], part), 2)
    both, arrived, grad_inner = lax.optimization_barrier((both, arrived, grad_inner))
    if rest > 1:
        arrived = jnp.sum(arrived.reshape(4, major, rest, shard, packed_width), axis=2)
        arrived = arrived.reshape(4 * major, shard, packed_width)
    grad_qk, grad_v, small = split_columns(arrived, major, heads, head_dim)
    summed = jnp.sum(small[:, :, : experts + 2], axis=0)
    grad_table = small[:, :, experts + 2 : experts + 2 + table_columns]
    grad_table = jnp.transpose(grad_table.reshape(major, buckets, heads), (1, 0, 2))
    grad_o = jnp.sum(grad_o.astype(F32), axis=0)
    grad_activations, layer_output = both[None, :rows], both[None, rows:]
    return (
        layer_output,
        grad_activations,
        grad_qk,
        grad_v,
        grad_o,
        summed[:, experts],
        summed[:, experts + 1],
        summed[:, :experts],
        grad_table.reshape(buckets, head_count),
        grad_inner,
        grad_outer,
    )


def solution(mesh):
    groups, ring = mesh.shape["exp"], mesh.shape["ctx"]
    split = Mesh(mesh.devices.reshape(groups // 2, 2, 2, 4, ring // 8), EVERY)
    exp, ctx = ("ey", "ec"), ("gh", "mj", "rs")
    tokens, rows, experts = P(exp, ctx, None), P(EVERY, None), P(ctx, exp, None)
    return jax.shard_map(
        per_device,
        mesh=split,
        in_specs=(
            tokens,
            tokens,
            rows,
            rows,
            rows,
            P(EVERY),
            P(EVERY),
            rows,
            P(),
            experts,
            experts,
            P(exp, ctx),
            P(exp, ctx),
        ),
        out_specs=(
            tokens,
            tokens,
            rows,
            rows,
            rows,
            P(EVERY),
            P(EVERY),
            rows,
            P(),
            experts,
            experts,
        ),
        check_vma=False,
    )
```

```python
import functools
import math

import jax
import jax.numpy as jnp
import numpy as np
from jax import lax
from jax.experimental import pallas as pl
from jax.experimental.pallas import tpu as pltpu
from jax.sharding import Mesh
from jax.sharding import PartitionSpec as P

EPS = 1e-06
F32 = jnp.float32
BF16 = jnp.bfloat16
EVERY = ("ey", "ec", "gh", "mj", "rs")
MINOR = ("ec", "rs")
REST = ("ey", "gh", "mj", "rs")
VMEM_BYTES = 56 * 1024 * 1024


def bucket_edges(reach):
    magnitude = np.arange(reach)
    spread = 8 + (np.log(np.maximum(magnitude, 1) / 8.0) / np.log(16.0) * 8.0).astype(np.int64)
    bucket = np.where(magnitude < 8, magnitude, np.minimum(spread, 15))
    return [int(np.argmax(bucket >= number)) for number in range(16)]


def dot_t(left, right):
    return lax.dot_general(left, right, (((1,), (1,)), ((), ())), preferred_element_type=F32)


def dot_0(left, right):
    return lax.dot_general(left, right, (((0,), (0,)), ((), ())), preferred_element_type=F32)


def dot_n(left, right):
    return jnp.dot(left, right, preferred_element_type=F32)


def near_bias_kernel(edges, rows, table_ref, out_ref):
    shape = (3 * rows, rows)
    relative = (
        lax.broadcasted_iota(jnp.int32, shape, 0) - rows - lax.broadcasted_iota(jnp.int32, shape, 1)
    )
    magnitude = jnp.abs(relative)
    ahead = relative > 0
    for head in range(out_ref.shape[0]):
        value = jnp.where(ahead, table_ref[16, head], table_ref[0, head])
        for number in range(1, 16):
            value = jnp.where(
                magnitude >= edges[number],
                jnp.where(ahead, table_ref[16 + number, head], table_ref[number, head]),
                value,
            )
        out_ref[head] = value


def bucket_sum_kernel(edges, rows, near_ref, far_ref, out_ref):
    shape = (3 * rows, rows)
    relative = (
        lax.broadcasted_iota(jnp.int32, shape, 0) - rows - lax.broadcasted_iota(jnp.int32, shape, 1)
    )
    magnitude = jnp.abs(relative)
    lanes = lax.broadcasted_iota(jnp.int32, (1, 128), 1)
    for head in range(near_ref.shape[0]):
        grads = near_ref[head]
        behind = jnp.where(relative > 0, 0.0, grads)
        forward = jnp.where(relative > 0, grads, 0.0)
        total = jnp.zeros((1, 128), F32)
        for side, part in enumerate((behind, forward)):
            for number in range(16):
                inside = magnitude >= edges[number]
                if number < 15:
                    inside = inside & (magnitude < edges[number + 1])
                value = jnp.sum(jnp.sum(jnp.where(inside, part, 0.0), axis=0, keepdims=True))
                if number == 15:
                    value = value + jnp.sum(far_ref[head, side : side + 1, :])
                total = jnp.where(lanes == side * 16 + number, value, total)
        out_ref[head : head + 1, :] = total


def biased_scores(parts, key_ref, place_ref, far_ref, near_ref, scratch, head, block, rows):
    pieces = [
        part[first : first + rows, :] for part in parts for first in range(0, part.shape[0], rows)
    ]
    slots = len(pieces)
    for slot in range(slots):
        far = jnp.where(
            key_ref[slot] < block - 1,
            far_ref[0, head],
            jnp.where(key_ref[slot] > block + 1, far_ref[1, head], 0.0),
        )
        scratch[slot * rows : (slot + 1) * rows, :] = pieces[slot] + far
    for step in range(3):
        window = pl.ds(pl.multiple_of(place_ref[block + step] * rows, rows), rows)
        scratch[window, :] = scratch[window, :] + near_ref[head, step * rows : (step + 1) * rows, :]
    return scratch[0 : slots * rows, :]


def head_queries(q_ref, heads, head):
    first = heads * 128 + head * 64
    query = q_ref[:, first : first + 64]
    return jnp.concatenate([query, jnp.zeros_like(query)], axis=1)


def attention_kernel(
    heads,
    rows,
    block_ref,
    key_ref,
    place_ref,
    far_ref,
    q_ref,
    own_ref,
    other_ref,
    near_ref,
    low_ref,
    wide_ref,
    lse_ref,
    scratch,
):
    block = block_ref[pl.program_id(0)]
    own_rows = own_ref.shape[0]
    for head in range(heads):
        lanes = slice(head * 128, (head + 1) * 128)
        own, other = own_ref[:, lanes], other_ref[:, lanes]
        query = head_queries(q_ref, heads, head)
        scores = biased_scores(
            (dot_t(own, query), dot_t(other, query)),
            key_ref,
            place_ref,
            far_ref,
            near_ref,
            scratch.at[head % scratch.shape[0]],
            head,
            block,
            rows,
        )
        top = jnp.max(scores, axis=0, keepdims=True)
        weights = jnp.exp(scores - top)
        total = jnp.sum(weights, axis=0, keepdims=True)
        low = (weights * (1.0 / total)).astype(BF16)
        result = dot_0(low[:own_rows], own) + dot_0(low[own_rows:], other)
        wide_ref[:, lanes] = result
        low_ref[:, head * 64 : (head + 1) * 64] = result[:, 64:].astype(BF16)
        lse_ref[0, head : head + 1, :] = top + jnp.log(total)


def attention_back_kernel(
    heads,
    rows,
    block_ref,
    key_ref,
    place_ref,
    far_ref,
    q_ref,
    g_ref,
    wide_ref,
    own_ref,
    other_ref,
    near_ref,
    lse_ref,
    dq_ref,
    sum_ref,
    low_ref,
    near_sum_ref,
    far_sum_ref,
    scratch,
    grad_scratch,
    total_scratch,
):
    step = pl.program_id(0)
    block = block_ref[step]
    own_rows = own_ref.shape[0]
    count = own_rows + other_ref.shape[0]
    slots = count // rows

    @pl.when(step == 0)
    def _():
        total_scratch[...] = jnp.zeros_like(total_scratch)
        near_sum_ref[...] = jnp.zeros_like(near_sum_ref)
        far_sum_ref[...] = jnp.zeros_like(far_sum_ref)
        for copy in range(grad_scratch.shape[0]):
            grad_scratch[copy, count : count + rows, :] = jnp.zeros((rows, rows), F32)

    for head in range(heads):
        copy = head % scratch.shape[0]
        lanes = slice(head * 128, (head + 1) * 128)
        own, other = own_ref[:, lanes], other_ref[:, lanes]
        grad = g_ref[:, head * 64 : (head + 1) * 64]
        grad = jnp.concatenate([jnp.zeros_like(grad), grad], axis=1)
        delta = jnp.sum(jnp.transpose(grad.astype(F32) * wide_ref[:, lanes]), axis=0, keepdims=True)
        both = jnp.concatenate([head_queries(q_ref, heads, head), grad], axis=0)
        first, second = dot_t(own, both), dot_t(other, both)
        scores = biased_scores(
            (first[:, :rows], second[:, :rows]),
            key_ref,
            place_ref,
            far_ref,
            near_ref,
            scratch.at[copy],
            head,
            block,
            rows,
        )
        chances = jnp.exp(scores - lse_ref[0, head : head + 1, :])
        products = jnp.concatenate([first[:, rows:], second[:, rows:]], axis=0)
        grads = chances * (products - delta)
        grads_low = grads.astype(BF16)
        grad_scratch[copy, 0:count, :] = grads
        for part in range(3):
            window = pl.ds(pl.multiple_of(place_ref[block + part] * rows, rows), rows)
            near_sum_ref[head, part * rows : (part + 1) * rows, :] += grad_scratch[copy, window, :]
        low_far = jnp.zeros((1, rows), F32)
        high_far = jnp.zeros((1, rows), F32)
        for slot in range(slots):
            line = jnp.sum(grads[slot * rows : (slot + 1) * rows, :], axis=0, keepdims=True)
            low_far = low_far + line * jnp.where(key_ref[slot] < block - 1, 1.0, 0.0)
            high_far = high_far + line * jnp.where(key_ref[slot] > block + 1, 1.0, 0.0)
        far_sum_ref[head, 0:1, :] += low_far
        far_sum_ref[head, 1:2, :] += high_far
        pair = jnp.concatenate([grads_low, chances.astype(BF16)], axis=1)
        total_scratch[:, lanes] += dot_n(pair, both)
        dq = dot_0(grads_low[:own_rows], own) + dot_0(grads_low[own_rows:], other)
        dq_ref[:, head * 64 : (head + 1) * 64] = dq[:, :64].astype(BF16)

    dq_ref[:, heads * 64 :] = jnp.zeros_like(dq_ref[:, heads * 64 :])

    @pl.when(step == pl.num_programs(0) - 1)
    def _():
        sum_ref[...] = total_scratch[0:own_rows, :]
        low_ref[...] = total_scratch[own_rows:count, :].astype(BF16)


def column_kernel(major, heads, size, in_ref, qk_ref, v_ref, small_ref):
    terms = in_ref.shape[0] // major
    for group in range(major):
        total = in_ref[group].astype(F32)
        for term in range(1, terms):
            total = total + in_ref[term * major + group].astype(F32)
        queries, start = heads * 2 * size, group * heads * size
        features = major * heads * size
        qk_ref[:, start : start + heads * size] = total[:, queries : queries + heads * size]
        for head in range(heads):
            first, place = head * 2 * size, start + head * size
            qk_ref[:, features + place : features + place + size] = total[:, first : first + size]
            v_ref[:, place : place + size] = total[:, first + size : first + 2 * size]
        small_ref[group] = total[:, queries + heads * size :]


def split_columns(value, major, heads, size):
    rows, columns = value.shape[1:]
    features = major * heads * size
    return pl.pallas_call(
        functools.partial(column_kernel, major, heads, size),
        out_shape=[
            jax.ShapeDtypeStruct((rows, 2 * features), F32),
            jax.ShapeDtypeStruct((rows, features), F32),
            jax.ShapeDtypeStruct((major, rows, columns - 3 * heads * size), F32),
        ],
    )(value)


def unpack_kernel(cuts, in_ref, out_ref):
    count = in_ref.shape[0]
    step = in_ref.shape[2] // cuts
    for cut in range(cuts):
        for index in range(count):
            first = (cut * count + index) * step
            value = in_ref[index, :, cut * step : (cut + 1) * step].astype(F32)
            out_ref[:, 0, first : first + step] = value


def unpack(value, cuts):
    count, rows, columns = value.shape
    return pl.pallas_call(
        functools.partial(unpack_kernel, cuts),
        out_shape=jax.ShapeDtypeStruct((rows, 1, count * columns), F32),
    )(value)


def whole_block(shape):
    zeros = (0,) * len(shape)
    return pl.BlockSpec(shape, lambda *_: zeros)


def scalars():
    return pl.BlockSpec(memory_space=pltpu.SMEM)


def slot_count(heads, count):
    return heads if count <= 2048 else 1


def estimate(products, steps, rows, count, heads):
    return pl.CostEstimate(
        flops=2 * products * steps * rows * count * heads * 128,
        bytes_accessed=1024 * count * heads,
        transcendentals=steps * rows * count * heads,
    )


def forward_attention(projected, other, near, far, places, heads, rows):
    steps = places[0].shape[0]
    own = steps * rows
    count = own + other.shape[0]
    width = heads * 128
    return pl.pallas_call(
        functools.partial(attention_kernel, heads, rows),
        grid=(steps,),
        in_specs=[scalars()] * 4
        + [
            pl.BlockSpec((rows, projected.shape[1]), lambda i: (i, 0)),
            whole_block((own, width)),
            whole_block((count - own, width)),
            whole_block(near.shape),
        ],
        out_specs=[
            pl.BlockSpec((rows, width // 2), lambda i: (i, 0)),
            pl.BlockSpec((rows, width), lambda i: (i, 0)),
            pl.BlockSpec((1, heads, rows), lambda i: (i, 0, 0)),
        ],
        out_shape=[
            jax.ShapeDtypeStruct((own, width // 2), BF16),
            jax.ShapeDtypeStruct((own, width), F32),
            jax.ShapeDtypeStruct((steps, heads, rows), F32),
        ],
        scratch_shapes=[pltpu.VMEM((slot_count(heads, count), count + rows, rows), F32)],
        compiler_params=pltpu.CompilerParams(vmem_limit_bytes=VMEM_BYTES),
        cost_estimate=estimate(2, steps, rows, count, heads),
    )(*places, far, projected, projected, other, near)


def backward_attention(projected, grads, wide, other, near, far, places, lse, heads, rows):
    steps = places[0].shape[0]
    own = steps * rows
    count = own + other.shape[0]
    width = heads * 128
    dq_width = -(-width // 256) * 128
    slots = slot_count(heads, count)
    return pl.pallas_call(
        functools.partial(attention_back_kernel, heads, rows),
        grid=(steps,),
        in_specs=[scalars()] * 4
        + [
            pl.BlockSpec((rows, projected.shape[1]), lambda i: (i, 0)),
            pl.BlockSpec((rows, width // 2), lambda i: (i, 0)),
            pl.BlockSpec((rows, width), lambda i: (i, 0)),
            whole_block((own, width)),
            whole_block((count - own, width)),
            whole_block(near.shape),
            pl.BlockSpec((1, heads, rows), lambda i: (i, 0, 0)),
        ],
        out_specs=[
            pl.BlockSpec((rows, dq_width), lambda i: (i, 0)),
            whole_block((own, width)),
            whole_block((count - own, width)),
            whole_block(near.shape),
            whole_block((heads, 2, rows)),
        ],
        out_shape=[
            jax.ShapeDtypeStruct((own, dq_width), BF16),
            jax.ShapeDtypeStruct((own, width), F32),
            jax.ShapeDtypeStruct((count - own, width), BF16),
            jax.ShapeDtypeStruct(near.shape, F32),
            jax.ShapeDtypeStruct((heads, 2, rows), F32),
        ],
        scratch_shapes=[
            pltpu.VMEM((slots, count + rows, rows), F32),
            pltpu.VMEM((slots, count + rows, rows), F32),
            pltpu.VMEM((count, width), F32),
        ],
        compiler_params=pltpu.CompilerParams(vmem_limit_bytes=VMEM_BYTES),
        cost_estimate=estimate(5, steps, rows, count, heads),
    )(*places, far, projected, grads, wide, projected, other, near, lse)


def swap(value, axis):
    return lax.ppermute(value, axis, [(0, 1), (1, 0)])


def turn(value):
    return lax.ppermute(value, ("ec", "gh"), [(0, 0), (1, 2), (2, 1), (3, 3)])


def exchange(parts, axis):
    count = len(parts)
    return [parts[0]] + [
        lax.ppermute(parts[step], axis, [(source, source ^ step) for source in range(count)])
        for step in range(1, count)
    ]


def ordered(value, place):
    count = value.shape[0]
    return jnp.take(value, jnp.arange(count) ^ place, axis=0, mode="clip")


def exchange_ordered(value, axis):
    place = lax.axis_index(axis)
    count = value.shape[0]
    parts = exchange(
        [lax.dynamic_index_in_dim(value, place ^ step, keepdims=False) for step in range(count)], axis
    )
    return ordered(jnp.stack(parts), place)


def turn_exchange(parts):
    arrived = []
    for step, part in enumerate(parts):
        pairs = []
        for source in range(8):
            ey, ec, gh = source // 4, source // 2 % 2, source % 2
            pairs.append((source, (ey ^ (step // 2)) * 4 + gh * 2 + (ec ^ (step % 2))))
        arrived.append(lax.ppermute(part, ("ey", "ec", "gh"), pairs))
    return arrived


def in_order(own, other, axis, place=0):
    first = lax.axis_index(axis) == 0
    return jnp.stack([jnp.where(first, own, other), jnp.where(first, other, own)], axis=place)


def gather_pair(value, axis, place=0):
    return in_order(value, swap(value, axis), axis, place)


def gather_minor(value):
    if lax.axis_size("rs") == 1:
        return gather_pair(value, "ec")
    return lax.all_gather(value, MINOR)


def nearest_first(value):
    count = value.shape[0]
    return jnp.take(value, jnp.arange(count) ^ lax.axis_index(MINOR), axis=0, mode="clip")


def other_minor(value, columns):
    if lax.axis_size("rs") == 1:
        return swap(value, "ec")
    return nearest_first(lax.all_gather(value[:, :columns], MINOR))[1:].reshape(-1, columns)


def sum_nearest(own, low):
    if lax.axis_size("rs") == 1:
        return own + swap(low[0], "ec").astype(F32)
    parts = nearest_first(jnp.concatenate([own.astype(BF16)[None], low]))
    return jnp.sum(lax.all_to_all(parts, MINOR, 0, 0, tiled=True).astype(F32), axis=0)


def split_minor(parts):
    if lax.axis_size("rs") != 1:
        return (parts.astype(BF16),)
    first = lax.axis_index("ec") == 0
    sent = jnp.where(first, parts[1], parts[0]).astype(BF16)
    return (jnp.where(first, parts[0], parts[1]), sent)


def sum_split(split):
    if lax.axis_size("rs") != 1:
        arrived = lax.all_to_all(split[0], MINOR, 0, 0, tiled=True)
        return jnp.sum(arrived.astype(F32), axis=0)
    return split[0] + swap(split[1], "ec").astype(F32)


def swap_major(value):
    return lax.all_to_all(value, "mj", 0, 0, tiled=True)


def core_sum(value):
    value = value.reshape(lax.axis_size("ey"), 2, -1, value.shape[1])
    first = lax.axis_index("ec") == 0
    sent = jnp.where(first, value[:, 1], value[:, 0]).astype(BF16)
    value = jnp.where(first, value[:, 0], value[:, 1]) + swap(sent, "ec").astype(F32)
    return value.astype(BF16)


def scatter_rows(value):
    chips = math.prod(lax.axis_size(name) for name in REST)
    value = value.reshape(chips, -1, value.shape[-1])
    return lax.all_to_all(value, REST, 0, 0, tiled=True)


def after(value, *others):
    return lax.optimization_barrier((value, others))[0]


def unit(hidden):
    return lax.rsqrt(jnp.mean(hidden * hidden, axis=-1, keepdims=True) + EPS)


def per_device(
    activations,
    cotangent,
    query_key_weight,
    value_weight,
    output_weight,
    norm_first,
    norm_second,
    router_weight,
    bias_table,
    w_in,
    w_out,
    routes,
    slots,
):
    rows, width = activations.shape[1:]
    major = lax.axis_size("mj")
    rest = lax.axis_size("rs")
    minor = 2 * rest
    ring = 2 * major * rest
    experts = router_weight.shape[1]
    capacity = rows * 5 // (4 * experts)
    head_count = bias_table.shape[1]
    heads = head_count // major
    features = value_weight.shape[1]
    head_dim = features // head_count
    shard = query_key_weight.shape[0]
    my_major = lax.axis_index("mj")
    my_exp = lax.axis_index(("ey", "gh"))
    edges = bucket_edges(4 * rows)
    kv_width = heads * 2 * head_dim
    q_width = heads * head_dim
    extra_width = 128 - (kv_width + q_width) % 128
    packed_width = kv_width + q_width + extra_width

    numbers = jnp.concatenate([routes, slots]).astype(BF16)
    numbers = jnp.pad(numbers, ((0, 14), (0, width - rows)))
    both = jnp.concatenate([activations[0], numbers])
    query_key_weight, value_weight, w_in = after((query_key_weight, value_weight, w_in), both)
    both = turn(both)
    tokens = both[:rows]
    numbers = both[rows : rows + 2, :rows].astype(jnp.int32)

    def by_head(value):
        return value.reshape(shard, major, heads, 1, head_dim)

    key_value = jnp.concatenate(
        [by_head(query_key_weight[:, features:]), by_head(value_weight)], axis=3
    ).reshape(shard, major, kv_width)
    extras = jnp.concatenate([router_weight, norm_first[:, None], norm_second[:, None]], axis=1)
    extras = jnp.pad(extras, ((0, 0), (0, extra_width - experts - 2)))
    packed = jnp.concatenate(
        [
            key_value,
            query_key_weight[:, :features].reshape(shard, major, q_width),
            jnp.broadcast_to(extras[:, None, :], (shard, major, extra_width)),
        ],
        axis=2,
    )
    packed = exchange_ordered(jnp.transpose(packed, (1, 0, 2)), "mj")
    column = exchange([tokens] * major, "mj")

    expert_ids = jnp.arange(experts, dtype=jnp.int32)
    slot_ids = jnp.arange(capacity, dtype=jnp.int32)

    def selection(token_routes, token_slots, place):
        chosen = (
            ((token_routes ^ place)[None, None, :] == expert_ids[:, None, None])
            & (token_slots[None, None, :] == slot_ids[None, :, None])
        ).astype(BF16)
        return chosen.reshape(experts * capacity, rows)

    def by_expert(chosen, value):
        sent = dot_n(chosen, value).astype(BF16)
        return [sent[i * capacity : (i + 1) * capacity] for i in range(experts)]

    sent = by_expert(selection(routes[0], slots[0], lax.axis_index(("ey", "ec"))), cotangent[0])
    cot_parts = turn_exchange(after(sent, packed))
    routes, slots = numbers[0], numbers[1]
    select = selection(routes, slots, my_exp)

    background = packed
    if rest == 1:
        packed = jnp.stack([packed, swap(packed, "gh")])
        background = packed
        packed = jnp.concatenate([packed, swap(packed, "ey")])
        packed, column, cot_parts = lax.optimization_barrier((packed, column, cot_parts))
        packed = ordered(packed, lax.axis_index(("ey", "gh"))).reshape(2, 2, major, shard, packed_width)
        packed = gather_pair(packed, "ec", 1)
    else:
        packed = lax.all_gather(packed, ("ey", "ec", "gh", "rs"))
        packed = packed.reshape(2, 2, 2, rest, major, shard, packed_width)
        packed = jnp.transpose(packed, (0, 1, 2, 4, 3, 5, 6))
    packed = packed.reshape(width, packed_width)
    extras = packed[:, kv_width + q_width :]
    full_router = extras[:, :experts]
    gain_first = extras[:, experts].astype(F32)
    gain_second = extras[:, experts + 1].astype(F32)

    column = jnp.stack(column)
    part = w_in.shape[2] // major
    half = part // 2
    inner = jnp.concatenate(
        [
            jnp.concatenate([w_in[:, 0, (side * major + i) * half :][:, :half] for side in range(2)], axis=1)
            for i in range(major)
        ]
    )
    inner = swap_major(inner.reshape(major, -1, part)).reshape(-1, part)
    both = jnp.concatenate([inner, w_out[:, 0, :], cotangent[0]])
    both = turn(after(both, background))

    full_o = lax.all_gather(output_weight, EVERY, axis=0, tiled=True)
    near_major = jnp.arange(major, dtype=jnp.int32) ^ my_major

    table = lax.dynamic_slice_in_dim(bias_table, my_major * heads, heads, axis=1).astype(F32)
    near = pl.pallas_call(
        functools.partial(near_bias_kernel, edges, rows),
        in_specs=[scalars()],
        out_shape=jax.ShapeDtypeStruct((heads, 3 * rows, rows), F32),
    )(table)
    far = jnp.stack([table[15], table[31]])
    near_minor = jnp.arange(minor, dtype=jnp.int32) ^ lax.axis_index(MINOR)
    key_blocks = (near_minor // rest)[:, None] * major + near_major[None, :]
    key_blocks = (key_blocks * rest + (near_minor % rest)[:, None]).reshape(-1)
    block_ids = jnp.arange(-1, ring + 1, dtype=jnp.int32)
    found = key_blocks[None, :] == block_ids[:, None]
    key_slots = jnp.where(found, jnp.arange(ring, dtype=jnp.int32)[None, :], 0)
    key_slots = jnp.where(jnp.any(found, axis=1), jnp.sum(key_slots, axis=1), ring)
    places = (key_blocks[:major], key_blocks, key_slots)

    def gather_rows(parts):
        return exchange([jnp.concatenate(parts)] * major, "mj")

    def in_parts(value):
        count = experts * capacity
        return [value[i * count : (i + 1) * count] for i in range(major)]

    def send_back(parts):
        total = sum(part.astype(F32) for part in parts).astype(BF16)
        total = total.reshape(experts, capacity, width)
        return exchange([total[i] for i in range(experts)], ("ey", "gh"))

    cot_rows = gather_rows(cot_parts)

    column_hidden = column.reshape(major * rows, width).astype(F32)
    column_unit = unit(column_hidden)
    normed = (column_hidden * column_unit * gain_first).astype(BF16)
    projected = dot_n(normed, packed).astype(BF16)
    others = other_minor(projected, kv_width)
    attended_low, attended_wide, lse = forward_attention(
        projected, others, near, far, places, heads, rows
    )
    attended_low, cot_rows = lax.optimization_barrier((attended_low, cot_rows))
    attended = exchange([attended_low[i * rows : (i + 1) * rows] for i in range(major)], "mj")
    attended = lax.optimization_barrier(attended)
    attended = lax.optimization_barrier(ordered(jnp.stack(attended), my_major))
    attended = jnp.concatenate([attended[i] for i in range(major)], axis=1)

    hidden = tokens.astype(F32)
    middle = hidden + dot_n(attended, full_o)
    middle_unit = unit(middle)
    mixed = (middle * middle_unit * gain_second).astype(BF16)
    chances = jax.nn.softmax(dot_n(mixed, full_router), axis=-1)
    route_mask = (routes[:, None] == expert_ids[None, :]).astype(F32)
    gate = jnp.sum(chances * route_mask, axis=-1, keepdims=True)
    mixed_parts = exchange(by_expert(select, mixed), ("ey", "gh"))
    both = after(both, attended)
    my_cotangent = both[-rows:]
    inner = both[: major * w_in.shape[0]]
    outer = gather_minor(both[major * w_in.shape[0] : -rows]).reshape(part, width)
    inner = gather_minor(inner.reshape(major, -1, part)).reshape(2, rest, major, -1, part)
    inner = jnp.transpose(inner, (0, 2, 1, 3, 4)).reshape(width, part)
    buffer = gather_rows(mixed_parts)
    cot_rows = jnp.concatenate(after(cot_rows, mixed_parts))
    buffer = jnp.concatenate(lax.optimization_barrier(buffer))
    row_chances = jax.nn.softmax(dot_n(buffer, full_router), axis=-1)
    row_mask = (expert_ids == my_exp).astype(F32)[None, :]
    row_gate = jnp.sum(row_chances * row_mask, axis=-1, keepdims=True)
    preact = dot_n(buffer, inner)
    cumulative = 0.5 * (1.0 + lax.erf(preact * math.sqrt(0.5)))
    density = jnp.exp(-0.5 * preact * preact) * (1.0 / math.sqrt(2.0 * math.pi))
    activated_wide = preact * cumulative
    grad_activated = dot_t(cot_rows, outer)
    grad_preact = (row_gate * grad_activated * (cumulative + preact * density)).astype(BF16)
    row_grad_gate = jnp.sum(activated_wide * grad_activated, axis=-1, keepdims=True)
    grad_logits = (row_gate * row_grad_gate * (row_mask - row_chances)).astype(BF16)
    grad_mixed = dot_t(grad_preact, inner) + dot_t(grad_logits, full_router)
    grad_mixed = grad_mixed.astype(BF16)
    buffer, activated_wide, grad_preact, cot_rows = after(
        (buffer, activated_wide, grad_preact, cot_rows), grad_mixed
    )

    activated = activated_wide.astype(BF16)
    produced = dot_n(activated, outer).astype(BF16)
    produced = in_parts(produced)
    grad_router = dot_0(buffer, grad_logits)
    gated_rows = (row_gate * cot_rows.astype(F32)).astype(BF16)
    grad_outer = dot_0(activated, gated_rows).reshape(minor, -1, width)
    grad_inner = dot_0(buffer, grad_preact).reshape(2, major, rest, -1, part)
    grad_inner = jnp.transpose(grad_inner, (0, 2, 1, 3, 4)).reshape(minor, -1, part)
    grad_outer, grad_inner, produced, grad_parts = lax.optimization_barrier(
        (split_minor(grad_outer), split_minor(grad_inner), produced, exchange(in_parts(grad_mixed), "mj"))
    )
    grad_parts = send_back(grad_parts)
    produced_parts = exchange(produced, "mj")
    grad_outer = sum_split(grad_outer).astype(BF16)
    grad_inner = sum_split(grad_inner).astype(BF16).reshape(major, -1, part)
    grad_parts, grad_outer, grad_inner = lax.optimization_barrier((grad_parts, grad_outer, grad_inner))
    grad_mixed = dot_0(select, jnp.concatenate(grad_parts))

    grad_z = my_cotangent.astype(F32)
    grad_gain_second = jnp.sum(grad_mixed * middle * middle_unit, axis=0)
    scaled = grad_mixed * gain_second
    grad_middle = (
        grad_z
        + middle_unit * scaled
        - middle * middle_unit**3 * jnp.mean(scaled * middle, axis=-1, keepdims=True)
    )
    grad_branch = grad_middle.astype(BF16)
    grad_attended = dot_t(grad_branch, full_o).astype(BF16)
    grad_attended = [
        lax.dynamic_slice_in_dim(grad_attended, (my_major ^ i) * q_width, q_width, axis=1)
        for i in range(major)
    ]
    grad_inner, grad_outer, attended, grad_branch = after(
        (grad_inner, grad_outer, attended, grad_branch), grad_attended
    )
    grad_attended = exchange(grad_attended, "mj")
    grad_attended = jnp.concatenate(lax.optimization_barrier(grad_attended))
    grad_outer = turn(grad_outer)
    grad_inner = swap_major(grad_inner).reshape(-1, part)
    grad_o = core_sum(dot_0(attended, grad_branch))

    dq, dkv, dkv_low, near_sum, far_sum = backward_attention(
        projected, grad_attended, attended_wide, others, near, far, places, lse, heads, rows
    )
    dq, dkv, dkv_low, grad_inner = lax.optimization_barrier((dq, dkv, dkv_low, grad_inner))
    grad_inner = turn(grad_inner)
    dkv = sum_nearest(dkv, dkv_low.reshape(minor - 1, major * rows, kv_width)).astype(BF16)
    grad_projected = jnp.concatenate([dkv, dq], axis=1)
    grad_normed = dot_t(grad_projected, packed)
    parts = grad_normed.astype(BF16).reshape(major, rows, width)
    produced_parts, near_sum, normed, grad_projected, grad_o, grad_outer = after(
        (produced_parts, near_sum, normed, grad_projected, grad_o, grad_outer), parts
    )
    produced_parts = send_back(produced_parts)
    grad_o = scatter_rows(grad_o)

    sums = pl.pallas_call(
        functools.partial(bucket_sum_kernel, edges, rows),
        out_shape=jax.ShapeDtypeStruct((heads, 128), F32),
    )(near_sum, far_sum)
    grad_table = sums[:, :32].T
    grad_gain_first = jnp.sum(grad_normed * column_hidden * column_unit, axis=0)
    grad_parts = exchange([parts[i] for i in range(major)], "mj")
    grad_outer = unpack(grad_outer[None], 1)
    grad_parts, grad_outer = lax.optimization_barrier((grad_parts, grad_outer))
    grad_normed = sum(part.astype(F32) for part in grad_parts)
    buckets = bias_table.shape[0]
    table_columns = buckets * heads // shard
    flat_table = jnp.tile(
        grad_table.reshape(shard, table_columns), (width // shard, 1)
    )
    small = jnp.concatenate(
        [grad_router, grad_gain_first[:, None], grad_gain_second[:, None], flat_table], axis=1
    )
    small = jnp.pad(small, ((0, 0), (kv_width + q_width, extra_width - small.shape[1])))
    grad_weight = core_sum(dot_0(normed, grad_projected) + small)
    produced = dot_0(select, jnp.concatenate(after(produced_parts, grad_normed, grad_weight)))
    layer_output = (middle + gate * produced).astype(BF16)
    hidden_unit = unit(hidden)
    scaled = grad_normed * gain_first
    grad_activations = (
        grad_middle
        + hidden_unit * scaled
        - hidden * hidden_unit**3 * jnp.mean(scaled * hidden, axis=-1, keepdims=True)
    ).astype(BF16)
    both = turn(jnp.concatenate([grad_activations, layer_output]))
    arrived = scatter_rows(grad_weight)
    grad_inner = unpack(grad_inner.reshape(major, w_in.shape[0], part), 2)
    both, arrived, grad_inner = lax.optimization_barrier((both, arrived, grad_inner))
    if rest > 1:
        arrived = jnp.sum(arrived.reshape(4, major, rest, shard, packed_width), axis=2)
        arrived = arrived.reshape(4 * major, shard, packed_width)
    grad_qk, grad_v, small = split_columns(arrived, major, heads, head_dim)
    summed = jnp.sum(small[:, :, : experts + 2], axis=0)
    grad_table = small[:, :, experts + 2 : experts + 2 + table_columns]
    grad_table = jnp.transpose(grad_table.reshape(major, buckets, heads), (1, 0, 2))
    grad_o = jnp.sum(grad_o.astype(F32), axis=0)
    grad_activations, layer_output = both[None, :rows], both[None, rows:]
    return (
        layer_output,
        grad_activations,
        grad_qk,
        grad_v,
        grad_o,
        summed[:, experts],
        summed[:, experts + 1],
        summed[:, :experts],
        grad_table.reshape(buckets, head_count),
        grad_inner,
        grad_outer,
    )


def solution(mesh):
    groups, ring = mesh.shape["exp"], mesh.shape["ctx"]
    split = Mesh(mesh.devices.reshape(groups // 2, 2, 2, 4, ring // 8), EVERY)
    exp, ctx = ("ey", "ec"), ("gh", "mj", "rs")
    tokens, rows, experts = P(exp, ctx, None), P(EVERY, None), P(ctx, exp, None)
    return jax.shard_map(
        per_device,
        mesh=split,
        in_specs=(
            tokens,
            tokens,
            rows,
            rows,
            rows,
            P(EVERY),
            P(EVERY),
            rows,
            P(),
            experts,
            experts,
            P(exp, ctx),
            P(exp, ctx),
        ),
        out_specs=(
            tokens,
            tokens,
            rows,
            rows,
            rows,
            P(EVERY),
            P(EVERY),
            rows,
            P(),
            experts,
            experts,
        ),
        check_vma=False,
    )
```
